256 devices in a mesh: dp: 4 (over x_lo, core), sample: 8 (over y, x_hi), head: 8 (over z).
Axes of the slice: x: 4 (x_hi: 2, x_lo: 2; x = x_hi * 2 + x_lo), y: 4, z: 8, core: 2. Of those that a mesh axis runs over, the one named last changes fastest.
Arguments:
- prompt_latent: bfloat16 [4, 512, 512], P('dp', ('sample', 'head')), may hold values from -6 to 6
- prompt_rope: bfloat16 [4, 512, 64], P('dp', ('sample', 'head')), may hold values from -6 to 6
- comp_latent: bfloat16 [4, 8, 256, 512], P('dp', 'sample'), may hold values from -6 to 6
- comp_rope: bfloat16 [4, 8, 256, 64], P('dp', 'sample'), may hold values from -6 to 6
- query_nope: bfloat16 [4, 8, 256, 16384], P('dp', 'sample', None, 'head'), may hold values from -6 to 6
- query_rope: bfloat16 [4, 8, 256, 8192], P('dp', 'sample', None, 'head'), may hold values from -100 to 100
- grad_out: bfloat16 [4, 8, 256, 16384], P('dp', 'sample', None, 'head'), may hold values from -48 to 48
- lengths: int32 [4, 8], P('dp', 'sample'), may hold values from 32 to 256, as said below
- w_uk: bfloat16 [512, 16384], P(None, 'head'), may hold values from -0.25 to 0.25
- w_uv: bfloat16 [512, 16384], P(None, 'head'), may hold values from -0.25 to 0.25
Outputs:
- grad_latent: float32 [4, 512, 512], P('dp', ('sample', 'head'))
- grad_rope: float32 [4, 512, 64], P('dp', ('sample', 'head'))
- grad_w_uk: float32 [512, 16384], P(('dp', 'sample'), 'head')
- grad_w_uv: float32 [512, 16384], P(('dp', 'sample'), 'head')
The draws below stay inside these ranges and needn't reach their ends.
Inputs may be any that keep to these rules, and one draw needn't show every extreme that they name: `lengths`: each prompt has one completion with all 256 slots live.
All inputs are finite; a program needn't handle non-finite values.
Results may differ from the reference program's by a relative error of at most 0.0097.
Values may be sent and summed in bfloat16 or wider, within the bound.
A program may use at most 128 MiB of HBM per device.

```python
import jax
import jax.numpy as jnp
from jax import lax

D_C = 512
DR = 64
DH = 128
HEADS = 128
PLEN = 512
CLEN = 256
PROMPTS = 4
SAMPLES = 8


def rope_base(key):
    first = jax.random.fold_in(key, 0)
    gauss = jax.random.normal(first, (PROMPTS, PLEN, DR), jnp.float32)
    own_rows = gauss
    own_rows = jnp.clip(own_rows, -6.0, 6.0)
    odd_rows = (jnp.arange(PLEN) % 2 == 1)[None, :, None]
    return jnp.where(odd_rows, own_rows, own_rows)


def draw_prompt_rope(key, part):
    shared = rope_base(key)
    return shared.astype(jnp.bfloat16)


def draw_query_rope(key, part):
    key = jax.random.fold_in(key, 2)
    result = jnp.clip(jax.random.normal(key, (PROMPTS, SAMPLES, CLEN, HEADS, DR), jnp.float32), -6.0, 6.0)
    return result.reshape(PROMPTS, SAMPLES, CLEN, HEADS * DR).astype(jnp.bfloat16)


def draw_lengths(key, part):
    key = jax.random.fold_in(key, 1)
    first, second = jax.random.split(key)
    drawn = jax.random.randint(first, (PROMPTS, SAMPLES), CLEN // 8, CLEN + 1)
    full_one = jax.random.randint(second, (PROMPTS,), 0, SAMPLES)
    chosen = jnp.arange(SAMPLES)[None, :] == full_one[:, None]
    return jnp.where(chosen, CLEN, drawn).astype(jnp.int32)


def block_scale(key, extent, cuts, smallest, largest):
    level, own = 1.0, jax.random.fold_in(key, 6)
    for position, blocks in cuts:
        draws = jnp.exp(jax.random.uniform(jax.random.fold_in(own, position), (blocks,), jnp.float32, smallest / len(cuts), largest / len(cuts)))
        level = level * jnp.repeat(draws, extent[position] // blocks).reshape([-1 if axis == position else 1 for axis in range(len(extent))])
    return level


def gaussian(key, dims, deviation, reach, cuts=(), held_as=jnp.bfloat16):
    gain = block_scale(key, dims, cuts, -0.22, 0.18) if cuts else 1.0
    entries = jax.random.normal(key, dims, jnp.float32) * deviation * gain
    return jnp.minimum(jnp.maximum(entries, -reach), reach).astype(held_as)


def setup_inputs(seed: int = 0) -> dict:
    seeds = jax.random.split(jax.random.key(seed), 11)
    prompt_latent = gaussian(seeds[0], (PROMPTS, PLEN, D_C), 1.0, 6.0, ((0, 4), (1, 64)))
    prompt_rope = draw_prompt_rope(jax.random.fold_in(seeds[10], 71), 0)
    comp_latent = gaussian(seeds[2], (PROMPTS, SAMPLES, CLEN, D_C), 1.0, 6.0, ((0, 4), (1, 8)))
    comp_rope = gaussian(seeds[3], (PROMPTS, SAMPLES, CLEN, DR), 1.0, 6.0, ((0, 4), (1, 8)))
    query_nope = gaussian(seeds[4], (PROMPTS, SAMPLES, CLEN, HEADS * DH), 1.0, 6.0, ((0, 4), (1, 8), (3, 8)))
    query_rope = draw_query_rope(jax.random.fold_in(seeds[10], 71), 0)
    grad_out = gaussian(seeds[6], (PROMPTS, SAMPLES, CLEN, HEADS * DH), 8.0, 48.0, ((0, 4), (1, 8), (3, 8)))
    lengths = draw_lengths(jax.random.fold_in(seeds[10], 71), 0)
    w_uk = gaussian(seeds[8], (D_C, HEADS * DH), D_C ** -0.5, 0.25, ((1, 8),))
    w_uv = gaussian(seeds[9], (D_C, HEADS * DH), D_C ** -0.5, 0.25, ((1, 8),))
    return dict(prompt_latent=prompt_latent, prompt_rope=prompt_rope, comp_latent=comp_latent, comp_rope=comp_rope, query_nope=query_nope, query_rope=query_rope, grad_out=grad_out, lengths=lengths, w_uk=w_uk, w_uv=w_uv)


def attend(query_nope, query_rope, grad_out, all_keys, all_values, all_rope, length):
    row_count = query_nope.shape[0]
    key_count = all_keys.shape[0]
    prompt_count = key_count - row_count
    score_scale = 1.0 / (query_nope.shape[2] + query_rope.shape[2]) ** 0.5
    score = jnp.einsum("rhd,khd->hrk", query_nope.astype(jnp.float32), all_keys.astype(jnp.float32))
    score = score + jnp.einsum("rhd,kd->hrk", query_rope.astype(jnp.float32), all_rope.astype(jnp.float32))
    score = score * score_scale
    row_index = jnp.arange(row_count, dtype=jnp.int32)[:, None]
    key_index = jnp.arange(key_count, dtype=jnp.int32)[None, :]
    visible = (key_index < prompt_count) | (key_index - prompt_count <= row_index)
    score = jnp.where(visible[None], score, -1e30)
    probs = jax.nn.softmax(score, axis=-1)
    probs_b = probs.astype(jnp.bfloat16)
    output = jnp.einsum("hrk,khd->rhd", probs_b.astype(jnp.float32), all_values.astype(jnp.float32))
    live_rows = (jnp.arange(row_count, dtype=jnp.int32) < length)[:, None, None]
    cotangent = jnp.where(live_rows, grad_out, jnp.zeros_like(grad_out))
    row_delta = jnp.sum(cotangent.astype(jnp.float32) * output, axis=-1)
    dprob = jnp.einsum("rhd,khd->hrk", cotangent.astype(jnp.float32), all_values.astype(jnp.float32))
    dscore = (probs * (dprob - row_delta.T[:, :, None])).astype(jnp.bfloat16)
    dkeys = (score_scale * jnp.einsum("hrk,rhd->khd", dscore.astype(jnp.float32), query_nope.astype(jnp.float32))).astype(jnp.bfloat16)
    drope = score_scale * jnp.einsum("hrk,rhd->kd", dscore.astype(jnp.float32), query_rope.astype(jnp.float32))
    dvalues = jnp.einsum("hrk,rhd->khd", probs_b.astype(jnp.float32), cotangent.astype(jnp.float32)).astype(jnp.bfloat16)
    return dkeys, dvalues, drope


def reference(prompt_latent, prompt_rope, comp_latent, comp_rope, query_nope, query_rope, grad_out, lengths, w_uk, w_uv):
    head_width = HEADS * DH

    def one_prompt(inputs):
        latent_p, rope_p, latent_c, rope_c, nope_c, qrope_c, cot_c, length_c = inputs
        keys_p = jnp.dot(latent_p, w_uk, preferred_element_type=jnp.float32).astype(jnp.bfloat16)
        values_p = jnp.dot(latent_p, w_uv, preferred_element_type=jnp.float32).astype(jnp.bfloat16)

        def one_sample(carry, sample):
            sum_k, sum_v, sum_rope, weight_comp = carry
            latent_s, rope_s, nope_s, qrope_s, cot_s, length_s = sample
            keys_c = jnp.dot(latent_s, w_uk, preferred_element_type=jnp.float32).astype(jnp.bfloat16)
            values_c = jnp.dot(latent_s, w_uv, preferred_element_type=jnp.float32).astype(jnp.bfloat16)
            all_keys = jnp.concatenate([keys_p, keys_c], 0).reshape(PLEN + CLEN, HEADS, DH)
            all_values = jnp.concatenate([values_p, values_c], 0).reshape(PLEN + CLEN, HEADS, DH)
            all_rope = jnp.concatenate([rope_p, rope_s], 0)
            dkeys, dvalues, drope = attend(nope_s.reshape(CLEN, HEADS, DH), qrope_s.reshape(CLEN, HEADS, DR),
                                           cot_s.reshape(CLEN, HEADS, DH), all_keys, all_values, all_rope, length_s)
            dkeys = dkeys.reshape(PLEN + CLEN, head_width)
            dvalues = dvalues.reshape(PLEN + CLEN, head_width)
            sum_k = sum_k + dkeys[:PLEN].astype(jnp.float32)
            sum_v = sum_v + dvalues[:PLEN].astype(jnp.float32)
            sum_rope = sum_rope + drope[:PLEN]
            comp_grads = jnp.concatenate([dkeys[PLEN:], dvalues[PLEN:]], 1)
            weight_comp = weight_comp + jnp.dot(latent_s.T, comp_grads, preferred_element_type=jnp.float32)
            return (sum_k, sum_v, sum_rope, weight_comp), None

        start = (jnp.zeros((PLEN, head_width), jnp.float32), jnp.zeros((PLEN, head_width), jnp.float32),
                 jnp.zeros((PLEN, DR), jnp.float32), jnp.zeros((D_C, 2 * head_width), jnp.float32))
        (sum_k, sum_v, sum_rope, weight_comp), _ = lax.scan(one_sample, start,
                                                           (latent_c, rope_c, nope_c, qrope_c, cot_c, length_c))
        latent_grad = jnp.dot(sum_k, w_uk.astype(jnp.float32).T, precision=lax.Precision.HIGHEST)
        latent_grad = latent_grad + jnp.dot(sum_v, w_uv.astype(jnp.float32).T, precision=lax.Precision.HIGHEST)
        weight_grad = jnp.dot(latent_p.astype(jnp.float32).T, jnp.concatenate([sum_k, sum_v], 1),
                              precision=lax.Precision.HIGHEST) + weight_comp
        return latent_grad, sum_rope, weight_grad

    grad_latent, grad_rope, weight_all = lax.map(one_prompt, (prompt_latent, prompt_rope, comp_latent, comp_rope,
                                                              query_nope, query_rope, grad_out, lengths))
    weight_sum = jnp.sum(weight_all, axis=0)
    return grad_latent, grad_rope, weight_sum[:, :head_width], weight_sum[:, head_width:]
```

```python
import math

import jax
import jax.numpy as jnp
from jax import lax
from jax.experimental import pallas as pl
from jax.experimental.pallas import tpu as pltpu
from jax.sharding import PartitionSpec as P

DH = 128
DR = 64
DC = 512
PLEN = 512
CLEN = 256
KEYS = PLEN + CLEN
WIDE = 640
PAIRS = 8
NT = (((1,), (1,)), ((), ()))
SCALE = 1.0 / (DH + DR) ** 0.5
F32 = jnp.float32
BF16 = jnp.bfloat16
MESH = pl.DeviceIdType.MESH


def remote(src, dst, send, recv, device):
    return pltpu.make_async_remote_copy(
        src_ref=src, dst_ref=dst, send_sem=send, recv_sem=recv, device_id=device, device_id_type=MESH
    )


def kernel(
    len_ref, plat_ref, prope_ref, clat_ref, crope_ref, q_ref, qr_ref, g_ref, wk_ref, wv_ref,
    glat_ref, grope_ref, gwk_ref, gwv_ref,
    gz, lat, lat_t, rsel, dkv, lacc, racc,
    wpart, crecv, csum, a1recv, a1sum, a2recv, b1recv, b1sum, b2recv,
    lpart, l1recv, l2src, l2recv, l3src, l3recv,
    gz_send, gz_recv, gx_send, gx_recv, gy_send, gy_recv,
    c_send, c_recv, a1_send, a1_recv, a2_send, a2_recv, b1_send, b1_recv, b2_send, b2_recv,
    l1_send, l1_recv, l2_send, l2_recv, l3_send, l3_recv,
):
    step = pl.program_id(0)
    dp, sample, z = lax.axis_index("dp"), lax.axis_index("sample"), lax.axis_index("head")
    x_lo, core = dp // 2, dp % 2
    y, x_hi = sample // 2, sample % 2
    x = x_hi * 2 + x_lo

    def at_core():
        return {"dp": x_lo * 2 + 1 - core}

    def at_x(d):
        to = (x + d) % 4
        return {"dp": (to % 2) * 2 + core, "sample": y * 2 + to // 2}

    def at_y(d):
        return {"sample": ((y + d) % 4) * 2 + x_hi}

    def at_z(d):
        return {"head": (z + d) % 8}

    def gather_z(d):
        return remote(gz.at[z], gz.at[z], gz_send.at[d - 1], gz_recv.at[d - 1], at_z(d))

    def gather_x():
        return remote(lat.at[sample], lat.at[sample], gx_send, gx_recv, at_x(2))

    def gather_y(d):
        mine = pl.ds(y * 2, 2)
        return remote(lat.at[mine], lat.at[mine], gy_send.at[d - 1], gy_recv.at[d - 1], at_y(d))

    def swap_core(i, lo):
        return remote(wpart.at[i, lo, 1 - core], crecv.at[i, lo], c_send.at[i, lo], c_recv.at[i, lo], at_core())

    def a_first(i, d):
        to = (x + d) % 4
        return remote(csum.at[i, 0, to % 2, :, to // 2], a1recv.at[i, d - 1], a1_send.at[i, d - 1], a1_recv.at[i, d - 1], at_x(d))

    def a_second(i, d):
        return remote(a1sum.at[i, (y + d) % 4], a2recv.at[i, d - 1], a2_send.at[i, d - 1], a2_recv.at[i, d - 1], at_y(d))

    def b_first(i, d):
        return remote(csum.at[i, 1, :, (y + d) % 4], b1recv.at[i, d - 1], b1_send.at[i, d - 1], b1_recv.at[i, d - 1], at_y(d))

    def b_second(i, d):
        to = (x + d) % 4
        return remote(b1sum.at[i, to % 2, to // 2], b2recv.at[i, d - 1], b2_send.at[i, d - 1], b2_recv.at[i, d - 1], at_x(d))

    def l_first(d):
        return remote(lpart.at[(y + d) % 4], l1recv.at[d - 1], l1_send.at[d - 1], l1_recv.at[d - 1], at_y(d))

    def l_second(d):
        return remote(l2src.at[(z + d) % 8], l2recv.at[d - 1], l2_send.at[d - 1], l2_recv.at[d - 1], at_z(d))

    def l_third():
        return remote(l3src.at[1 - x_hi], l3recv, l3_send, l3_recv, at_x(2))

    @pl.when(step == 0)
    def _():
        barrier = pltpu.get_barrier_semaphore()
        peers = [at_core()] + [at_x(d) for d in (1, 2, 3)] + [at_y(d) for d in (1, 2, 3)] + [at_z(d) for d in range(1, 8)]
        for peer in peers:
            pl.semaphore_signal(barrier, inc=1, device_id=peer, device_id_type=MESH)
        wide = jnp.concatenate(
            [plat_ref[...].astype(F32), prope_ref[...].astype(F32), jnp.zeros((8, 768 - DC - DR), F32)], 1
        )
        gz[z] = jnp.concatenate([wide[:, :384], wide[:, 384:]], 0).astype(BF16)
        pl.semaphore_wait(barrier, len(peers))
        for d in range(1, 8):
            gather_z(d).start()
        lat[pl.ds(8, 4), :, :DC] = clat_ref[...].reshape(4, 64, DC)
        lat[pl.ds(8, 4), :, DC:] = jnp.concatenate(
            [crope_ref[...], jnp.zeros((CLEN, WIDE - DC - DR), BF16)], 1
        ).reshape(4, 64, WIDE - DC)
        lacc[...] = jnp.zeros_like(lacc)
        racc[...] = jnp.zeros_like(racc)
        for d in range(1, 8):
            gather_z(d).wait()
        block = gz[...].astype(F32)
        lat[sample] = jnp.concatenate([block[:, :8], block[:, 8:, : WIDE - 384]], 2).reshape(64, WIDE).astype(BF16)
        gather_x().start()
        gather_x().wait()
        for d in (1, 2, 3):
            gather_y(d).start()
        for d in (1, 2, 3):
            gather_y(d).wait()
        rows = lat[...].reshape(KEYS, WIDE)
        lat_t[...] = rows[:, :DC].T
        rsel[0] = rows[:, DC:]
        rsel[1] = jnp.concatenate([jnp.zeros((KEYS, DR), BF16), rows[:, DC : DC + DR]], 1)

    @pl.when((step >= 1) & (step < PAIRS + 1))
    def _():
        i = step - 1
        for lo in range(2):
            swap_core(i, lo).wait()
        for half in range(2):
            for lo in range(2):
                csum[i, half, lo] = (
                    wpart[i, lo, core, half].astype(F32) + crecv[i, lo, half].astype(F32)
                ).astype(BF16)
        for d in (1, 2, 3):
            a_first(i, d).start()
            b_first(i, d).start()

    @pl.when((step >= 2) & (step < PAIRS + 2))
    def _():
        i = step - 2
        for d in (1, 2, 3):
            a_first(i, d).wait()
            b_first(i, d).wait()
        a = csum[i, 0, x_lo, :, x_hi].astype(F32)
        b = csum[i, 1, :, y].astype(F32)
        for d in range(3):
            a = a + a1recv[i, d].astype(F32)
            b = b + b1recv[i, d].astype(F32)
        a1sum[i] = a.astype(BF16)
        b1sum[i] = b.astype(BF16)
        for d in (1, 2, 3):
            a_second(i, d).start()
            b_second(i, d).start()

    @pl.when(step >= 3)
    def _():
        i = step - 3
        for d in (1, 2, 3):
            a_second(i, d).wait()
            b_second(i, d).wait()
        a = a1sum[i, y].astype(F32)
        b = b1sum[i, x_lo, x_hi].astype(F32)
        for d in range(3):
            a = a + a2recv[i, d].astype(F32)
            b = b + b2recv[i, d].astype(F32)
        cols = pl.ds(pl.multiple_of(i * 256, 256), 256)
        gwk_ref[:, cols] = a
        gwv_ref[:, cols] = b

    @pl.when(step == PAIRS)
    def _():
        for d in (1, 2, 3):
            l_first(d).wait()
        total = lpart[y].astype(F32)
        for d in range(3):
            total = total + l1recv[d].astype(F32)
        total = total.reshape(2, 8, 8, WIDE)
        l2src[...] = jnp.concatenate([total[0], total[1]], 1).astype(BF16)
        for d in range(1, 8):
            l_second(d).start()

    @pl.when(step == PAIRS + 1)
    def _():
        for d in range(1, 8):
            l_second(d).wait()
        total = l2src[z].astype(F32)
        for d in range(7):
            total = total + l2recv[d].astype(F32)
        l3src[...] = total.reshape(2, 8, WIDE)
        l_third().start()

    @pl.when(step == PAIRS + 2)
    def _():
        l_third().wait()
        total = l3src[x_hi] + l3recv[...]
        glat_ref[...] = total[:, :DC]
        grope_ref[...] = total[:, DC : DC + DR]

    @pl.when(step < PAIRS)
    def _():
        live = lax.broadcasted_iota(jnp.int32, (CLEN, 256), 0) < len_ref[0, 0]
        g = jnp.where(live, g_ref[...], jnp.zeros((), BF16))
        rows = lat[:, :, :DC].reshape(KEYS, DC)
        keys = jnp.dot(rows, wk_ref[...], preferred_element_type=F32).astype(BF16)
        vals = jnp.dot(rows, wv_ref[...], preferred_element_type=F32).astype(BF16)
        qr = qr_ref[...]
        see = lax.broadcasted_iota(jnp.int32, (CLEN, CLEN), 0) <= lax.broadcasted_iota(jnp.int32, (CLEN, CLEN), 1)
        for h in range(2):
            cols = slice(h * DH, (h + 1) * DH)
            kx = jnp.concatenate([keys[:, cols], rsel[h]], 1)
            qx = jnp.concatenate([q_ref[:, cols], qr], 1)
            gh = g[:, cols]
            s = lax.dot_general(kx, qx, NT, preferred_element_type=F32)
            s = jnp.concatenate([s[:PLEN], jnp.where(see, s[PLEN:], -1e30)], 0)
            m = jnp.max(s, axis=0, keepdims=True)
            p = jnp.exp2((s - m) * (SCALE * math.log2(math.e)))
            p = p * (1.0 / jnp.sum(p, axis=0, keepdims=True))
            pb = p.astype(BF16)
            dprob = lax.dot_general(vals[:, cols], gh, NT, preferred_element_type=F32)
            delta = jnp.sum(pb.astype(F32) * dprob, axis=0, keepdims=True)
            ds = (p * (dprob - delta)).astype(BF16)
            dk = jnp.dot(ds, qx, preferred_element_type=F32)
            dkv[0, :, cols] = (dk[:, :DH] * SCALE).astype(BF16)
            racc[h] += dk[:PLEN, DH:]
            dkv[1, :, cols] = jnp.dot(pb, gh, preferred_element_type=F32).astype(BF16)
        for half in range(2):
            part = jnp.dot(lat_t[...], dkv[half], preferred_element_type=F32).astype(BF16)
            part = part.reshape(2, 2, 4, 2, 16, 256)
            wpart[step, :, :, half] = part
        for lo in range(2):
            swap_core(step, lo).start()
        lacc[...] += lax.dot_general(dkv[0, :PLEN], wk_ref[...], NT, preferred_element_type=F32)
        lacc[...] += lax.dot_general(dkv[1, :PLEN], wv_ref[...], NT, preferred_element_type=F32)

    @pl.when(step == PAIRS - 1)
    def _():
        lpart[:, :, :DC] = lacc[...].astype(BF16).reshape(4, 128, DC)
        rope = (racc[0, :, :DR] + racc[1, :, DR:]) * SCALE
        rope = jnp.concatenate([rope, jnp.zeros((PLEN, WIDE - DC - DR), F32)], 1)
        lpart[:, :, DC:] = rope.astype(BF16).reshape(4, 128, WIDE - DC)
        for d in (1, 2, 3):
            l_first(d).start()

    @pl.when(step == PAIRS + 2)
    def _():
        pass


def local(prompt_latent, prompt_rope, comp_latent, comp_rope, query_nope, query_rope, grad_out, lengths, w_uk, w_uv):
    def whole(*shape):
        return pl.BlockSpec(shape, lambda i: (0,) * len(shape))

    def part(rows, cols):
        return pl.BlockSpec((rows, cols), lambda i: (0, jnp.minimum(i, PAIRS - 1)))

    dma = pltpu.SemaphoreType.DMA
    outs = pl.pallas_call(
        kernel,
        grid=(PAIRS + 3,),
        in_specs=[
            pl.BlockSpec(memory_space=pltpu.SMEM),
            whole(8, DC), whole(8, DR), whole(CLEN, DC), whole(CLEN, DR),
            part(CLEN, 256), part(CLEN, 128), part(CLEN, 256), part(DC, 256), part(DC, 256),
        ],
        out_specs=[whole(8, DC), whole(8, DR), whole(16, 2048), whole(16, 2048)],
        out_shape=[
            jax.ShapeDtypeStruct((8, DC), F32), jax.ShapeDtypeStruct((8, DR), F32),
            jax.ShapeDtypeStruct((16, 2048), F32), jax.ShapeDtypeStruct((16, 2048), F32),
        ],
        scratch_shapes=[
            pltpu.VMEM((8, 16, 384), BF16), pltpu.VMEM((12, 64, WIDE), BF16), pltpu.VMEM((DC, KEYS), BF16),
            pltpu.VMEM((2, KEYS, DH), BF16), pltpu.VMEM((2, KEYS, 256), BF16),
            pltpu.VMEM((PLEN, DC), F32), pltpu.VMEM((2, PLEN, 128), F32),
            pltpu.VMEM((PAIRS, 2, 2, 2, 4, 2, 16, 256), BF16),
            pltpu.VMEM((PAIRS, 2, 2, 4, 2, 16, 256), BF16),
            pltpu.VMEM((PAIRS, 2, 2, 4, 2, 16, 256), BF16),
            pltpu.VMEM((PAIRS, 3, 4, 16, 256), BF16), pltpu.VMEM((PAIRS, 4, 16, 256), BF16),
            pltpu.VMEM((PAIRS, 3, 16, 256), BF16),
            pltpu.VMEM((PAIRS, 3, 2, 2, 16, 256), BF16), pltpu.VMEM((PAIRS, 2, 2, 16, 256), BF16),
            pltpu.VMEM((PAIRS, 3, 16, 256), BF16),
            pltpu.VMEM((4, 128, WIDE), BF16), pltpu.VMEM((3, 128, WIDE), BF16),
            pltpu.VMEM((8, 16, WIDE), BF16), pltpu.VMEM((7, 16, WIDE), BF16),
            pltpu.VMEM((2, 8, WIDE), F32), pltpu.VMEM((8, WIDE), F32),
            dma((7,)), dma((7,)), dma, dma, dma((3,)), dma((3,)),
            dma((PAIRS, 2)), dma((PAIRS, 2)),
            dma((PAIRS, 3)), dma((PAIRS, 3)), dma((PAIRS, 3)), dma((PAIRS, 3)),
            dma((PAIRS, 3)), dma((PAIRS, 3)), dma((PAIRS, 3)), dma((PAIRS, 3)),
            dma((3,)), dma((3,)), dma((7,)), dma((7,)), dma, dma,
        ],
        compiler_params=pltpu.CompilerParams(
            vmem_limit_bytes=56 * 1024 * 1024, collective_id=0, has_side_effects=True
        ),
        cost_estimate=pl.CostEstimate(flops=13_000_000_000, bytes_accessed=8_000_000, transcendentals=3_200_000),
        name="mla_backward",
    )(
        lengths, prompt_latent[0], prompt_rope[0], comp_latent[0, 0], comp_rope[0, 0],
        query_nope[0, 0], query_rope[0, 0], grad_out[0, 0], w_uk, w_uv,
    )
    return (outs[0][None], outs[1][None], outs[2], outs[3])


def solution(mesh):
    in_specs = (
        P("dp", ("sample", "head"), None),
        P("dp", ("sample", "head"), None),
        P("dp", "sample", None, None),
        P("dp", "sample", None, None),
        P("dp", "sample", None, "head"),
        P("dp", "sample", None, "head"),
        P("dp", "sample", None, "head"),
        P("dp", "sample"),
        P(None, "head"),
        P(None, "head"),
    )
    out_specs = (
        P("dp", ("sample", "head"), None),
        P("dp", ("sample", "head"), None),
        P(("dp", "sample"), "head"),
        P(("dp", "sample"), "head"),
    )
    return jax.shard_map(local, mesh=mesh, in_specs=in_specs, out_specs=out_specs, check_vma=False)
```

```python
import math

import jax
import jax.numpy as jnp
from jax import lax
from jax.experimental import pallas as pl
from jax.experimental.pallas import tpu as pltpu
from jax.sharding import PartitionSpec as P

DH = 128
DR = 64
DC = 512
PLEN = 512
CLEN = 256
KEYS = PLEN + CLEN
WIDE = 640
PACK = 384
PAIRS = 8
NT = (((1,), (1,)), ((), ()))
SCALE = 1.0 / (DH + DR) ** 0.5
F32 = jnp.float32
BF16 = jnp.bfloat16
MESH = pl.DeviceIdType.MESH
OVER_XY = ((0, 0), (2, 0), (0, 1), (0, 3), (2, 1), (2, 3), (0, 2), (2, 2))
OVER_Z = (0, 1, 7, 2, 6, 3, 5, 4)
ALL_XY = tuple((dx, dy) for dx in range(4) for dy in range(4) if dx or dy)


def kernel(
    len_ref, plat_hbm, prope_hbm, clat_hbm, crope_hbm, q_hbm, qr_hbm, g_hbm, wk_hbm, wv_hbm,
    glat_ref, gw_ref,
    plat, prope, clat, crope, q_ref, qr_ref, g_ref, wk_ref, wv_ref,
    gz, lat, lat_t, rsel, kv, dkv, lacc, racc,
    wpart, crecv, csum, drecv, lpart, l1recv, l2src, l2own, l2recv,
    load, gz_send, gz_recv, gy_send, gy_recv, c_send, c_recv, d_send, d_recv, l1_send, l1_recv, l2_send, l2_recv,
):
    step = pl.program_id(0)
    dp, sample, z = lax.axis_index("dp"), lax.axis_index("sample"), lax.axis_index("head")
    x_lo, core = dp // 2, dp % 2
    y, x_hi = sample // 2, sample % 2
    x = x_hi * 2 + x_lo

    def at_xy(dx, dy):
        to = (x + dx) % 4
        return {"dp": (to % 2) * 2 + core, "sample": ((y + dy) % 4) * 2 + to // 2}

    def at_z(d):
        return {"head": (z + d) % 8}

    other_core = {"dp": x_lo * 2 + 1 - core}

    def remote(src, dst, send, recv, device):
        return pltpu.make_async_remote_copy(
            src_ref=src, dst_ref=dst, send_sem=send, recv_sem=recv, device_id=device, device_id_type=MESH
        )

    def arrived(ref, sem):
        pltpu.make_async_copy(ref, ref, sem).wait()

    def swap_core(i):
        return remote(wpart.at[i, :, 1 - core], crecv.at[i], c_send.at[i], c_recv.at[i], other_core)

    def project(first, count):
        rows = lat[first : first + count, :, :DC].reshape(count * 64, DC)

        def pair(i, carry):
            cols = pl.ds(pl.multiple_of(i * 256, 256), 256)
            for half, w in enumerate((wk_ref, wv_ref)):
                kv[i, half, first * 64 : (first + count) * 64] = jnp.dot(
                    rows, w[:, cols], preferred_element_type=F32
                ).astype(BF16)
            return carry

        lax.fori_loop(0, PAIRS, pair, 0)
        tokens = slice(first * 64, (first + count) * 64)
        lat_t[:, tokens] = rows.T
        rope = lat[first : first + count, :, DC:].reshape(count * 64, DH)
        rsel[0, tokens] = rope
        rsel[1, tokens] = jnp.concatenate([jnp.zeros((count * 64, DR), BF16), rope[:, :DR]], 1)

    @pl.when(step == 0)
    def _():
        pairs = (
            (plat_hbm, plat), (prope_hbm, prope), (clat_hbm, clat), (crope_hbm, crope), (wk_hbm, wk_ref),
            (wv_hbm, wv_ref), (q_hbm, q_ref), (qr_hbm, qr_ref), (g_hbm, g_ref),
        )
        loads = [pltpu.make_async_copy(src, dst, load.at[n]) for n, (src, dst) in enumerate(pairs)]
        for copy in loads:
            copy.start()
        barrier = pltpu.get_barrier_semaphore()
        peers = [other_core] + [at_xy(dx, dy) for dx, dy in ALL_XY] + [at_z(d) for d in range(1, 8)]
        for peer in peers:
            pl.semaphore_signal(barrier, inc=1, device_id=peer, device_id_type=MESH)
        loads[0].wait()
        loads[1].wait()
        wide = jnp.concatenate([plat[...].astype(F32), prope[...].astype(F32), jnp.zeros((8, 2 * PACK - DC - DR), F32)], 1)
        gz[0] = jnp.concatenate([wide[:, :PACK], wide[:, PACK:]], 0).astype(BF16)
        pl.semaphore_wait(barrier, len(peers))
        for k in range(1, 8):
            remote(gz.at[0], gz.at[k], gz_send, gz_recv, at_z(8 - OVER_Z[k])).start()
        loads[2].wait()
        loads[3].wait()
        lat[8:12, :, :DC] = clat[...].reshape(4, 64, DC)
        rope = jnp.concatenate([crope[...].astype(F32).T, jnp.zeros((CLEN, WIDE - DC - DR), F32)], 1)
        lat[8:12, :, DC:] = rope.astype(BF16).reshape(4, 64, WIDE - DC)
        lacc[...] = jnp.zeros_like(lacc)
        racc[...] = jnp.zeros_like(racc)
        loads[4].wait()
        loads[5].wait()
        project(8, 4)
        arrived(gz.at[pl.ds(1, 7)], gz_recv)
        block = gz[...].astype(F32)
        lat[0] = jnp.concatenate([block[:, :8], block[:, 8:, : WIDE - PACK]], 2).reshape(64, WIDE).astype(BF16)
        for b in range(1, 8):
            dx, dy = OVER_XY[b]
            remote(lat.at[0], lat.at[b], gy_send, gy_recv.at[b // 4], at_xy(4 - dx, 4 - dy)).start()
        for copy in loads[6:]:
            copy.wait()
        live = lax.broadcasted_iota(jnp.int32, g_ref.shape, 0) < len_ref[0, 0]
        g_ref[...] = jnp.where(live, g_ref[...], jnp.zeros((), BF16))
        arrived(lat.at[pl.ds(1, 3)], gy_recv.at[0])
        project(0, 4)
        arrived(lat.at[pl.ds(4, 4)], gy_recv.at[1])
        project(4, 4)
        arrived(gz.at[pl.ds(1, 7)], gz_send)
        arrived(lat.at[pl.ds(1, 7)], gy_send)

    @pl.when(step < PAIRS)
    def _():
        pair = pl.ds(pl.multiple_of(step * 256, 256), 256)
        qr = qr_ref[:, pl.ds(pl.multiple_of(step * DH, DH), DH)]
        see = lax.broadcasted_iota(jnp.int32, (CLEN, CLEN), 0) <= lax.broadcasted_iota(jnp.int32, (CLEN, CLEN), 1)
        keys, vals = kv[step, 0], kv[step, 1]
        q, g = q_ref[:, pair], g_ref[:, pair]
        for h in range(2):
            cols = slice(h * DH, (h + 1) * DH)
            kx = jnp.concatenate([keys[:, cols], rsel[h]], 1)
            qx = jnp.concatenate([q[:, cols], qr], 1)
            gh = g[:, cols]
            s = lax.dot_general(kx, qx, NT, preferred_element_type=F32)
            s = jnp.concatenate([s[:PLEN], jnp.where(see, s[PLEN:], -1e30)], 0)
            m = jnp.max(s, axis=0, keepdims=True)
            p = jnp.exp2((s - m) * (SCALE * math.log2(math.e)))
            p = p * (1.0 / jnp.sum(p, axis=0, keepdims=True))
            pb = p.astype(BF16)
            dprob = lax.dot_general(vals[:, cols], gh, NT, preferred_element_type=F32)
            delta = jnp.sum(pb.astype(F32) * dprob, axis=0, keepdims=True)
            ds = (p * (dprob - delta)).astype(BF16)
            dk = jnp.dot(ds, qx, preferred_element_type=F32)
            dkv[:, cols] = (dk[:, :DH] * SCALE).astype(BF16)
            racc[h] += dk[:PLEN, DH:]
            dkv[:, 256 + h * DH : 256 + (h + 1) * DH] = jnp.dot(pb, gh, preferred_element_type=F32).astype(BF16)
        both = jnp.concatenate([wk_ref[:, pair], wv_ref[:, pair]], 1)
        lacc[...] += lax.dot_general(dkv[:PLEN], both, NT, preferred_element_type=F32)

    @pl.when(step == PAIRS - 1)
    def _():
        lpart[:, :, :DC] = lacc[...].astype(BF16).reshape(8, 64, DC)
        rope = (racc[0, :, :DR] + racc[1, :, DR:]) * SCALE
        rope = jnp.concatenate([rope, jnp.zeros((PLEN, WIDE - DC - DR), F32)], 1)
        lpart[:, :, DC:] = rope.astype(BF16).reshape(8, 64, WIDE - DC)
        for b in range(1, 8):
            remote(lpart.at[b], l1recv.at[b - 1], l1_send, l1_recv, at_xy(*OVER_XY[b])).start()

    @pl.when((step >= 1) & (step < PAIRS + 1))
    def _():
        i = step - 1
        swap_core(i).wait()
        for lo in range(2):
            csum[i, lo] = (wpart[i, lo, core].astype(F32) + crecv[i, lo].astype(F32)).astype(BF16)
        for n, (dx, dy) in enumerate(ALL_XY):
            to = (x + dx) % 4
            remote(
                csum.at[i, to % 2, (y + dy) % 4, to // 2], drecv.at[i, n], d_send.at[i], d_recv.at[i], at_xy(dx, dy)
            ).start()

    @pl.when(step < PAIRS)
    def _():
        part = jnp.dot(lat_t[...], dkv[...], preferred_element_type=F32).astype(BF16)
        wpart[step] = part.reshape(2, 2, 4, 2, 16, 512)
        swap_core(step).start()

    @pl.when(step >= 2)
    def _():
        i = step - 2
        arrived(drecv.at[i], d_recv.at[i])
        total = csum[i, x_lo, y, x_hi].astype(F32)
        for n in range(15):
            total = total + drecv[i, n].astype(F32)
        cols = pl.ds(pl.multiple_of(i * 256, 256), 256)
        gw_ref[0, :, cols] = total[:, :256]
        gw_ref[1, :, cols] = total[:, 256:]
        arrived(drecv.at[i], d_send.at[i])

    @pl.when(step == PAIRS)
    def _():
        arrived(l1recv, l1_recv)
        total = lpart[0].astype(F32)
        for b in range(7):
            total = total + l1recv[b].astype(F32)
        total = jnp.concatenate([total, jnp.zeros((64, 2 * PACK - WIDE), F32)], 1).reshape(8, 8, 2 * PACK)
        total = jnp.concatenate([total[:, :, :PACK], total[:, :, PACK:]], 1)
        l2own[...] = total[0]
        l2src[...] = total.astype(BF16)
        for k in range(1, 8):
            remote(l2src.at[k], l2recv.at[k - 1], l2_send, l2_recv, at_z(OVER_Z[k])).start()

    @pl.when(step == PAIRS + 1)
    def _():
        arrived(l2recv, l2_recv)
        total = l2own[...]
        for k in range(7):
            total = total + l2recv[k].astype(F32)
        glat_ref[...] = jnp.concatenate([total[:8], total[8:, : WIDE - PACK]], 1)
        arrived(l1recv, l1_send)
        arrived(l2recv, l2_send)


def finish(lat_ref, w_ref, glat_ref, grope_ref, gwk_ref, gwv_ref):
    glat_ref[...] = lat_ref[:, :DC]
    grope_ref[...] = lat_ref[:, DC : DC + DR]
    gwk_ref[...] = w_ref[0]
    gwv_ref[...] = w_ref[1]


def local(prompt_latent, prompt_rope, comp_latent, comp_rope, query_nope, query_rope, grad_out, lengths, w_uk, w_uv):
    def whole(*shape):
        return pl.BlockSpec(shape, lambda i: (0,) * len(shape))

    vmem, dma = pltpu.VMEM, pltpu.SemaphoreType.DMA
    lat, weights = pl.pallas_call(
        kernel,
        grid=(PAIRS + 2,),
        in_specs=[pl.BlockSpec(memory_space=pltpu.SMEM)] + [pl.BlockSpec(memory_space=pl.ANY)] * 9,
        out_specs=[whole(8, WIDE), whole(2, 16, 2048)],
        out_shape=[jax.ShapeDtypeStruct((8, WIDE), F32), jax.ShapeDtypeStruct((2, 16, 2048), F32)],
        scratch_shapes=[
            vmem((8, DC), BF16), vmem((8, DR), BF16), vmem((CLEN, DC), BF16), vmem((DR, CLEN), BF16),
            vmem((CLEN, 2048), BF16), vmem((CLEN, 1024), BF16), vmem((CLEN, 2048), BF16),
            vmem((DC, 2048), BF16), vmem((DC, 2048), BF16),
            vmem((8, 16, PACK), BF16), vmem((12, 64, WIDE), BF16), vmem((DC, KEYS), BF16), vmem((2, KEYS, DH), BF16),
            vmem((PAIRS, 2, KEYS, 256), BF16), vmem((KEYS, 512), BF16), vmem((PLEN, DC), F32), vmem((2, PLEN, DH), F32),
            vmem((PAIRS, 2, 2, 4, 2, 16, 512), BF16),
            vmem((PAIRS, 2, 4, 2, 16, 512), BF16), vmem((PAIRS, 2, 4, 2, 16, 512), BF16),
            vmem((PAIRS, 15, 16, 512), BF16),
            vmem((8, 64, WIDE), BF16), vmem((7, 64, WIDE), BF16),
            vmem((8, 16, PACK), BF16), vmem((16, PACK), F32), vmem((7, 16, PACK), BF16),
            dma((9,)), dma, dma, dma, dma((2,)), dma((PAIRS,)), dma((PAIRS,)), dma((PAIRS,)), dma((PAIRS,)),
            dma, dma, dma, dma,
        ],
        compiler_params=pltpu.CompilerParams(
            vmem_limit_bytes=56 * 1024 * 1024, collective_id=0, has_side_effects=True
        ),
        cost_estimate=pl.CostEstimate(flops=13_000_000_000, bytes_accessed=8_000_000, transcendentals=3_200_000),
        name="mla_backward",
    )(
        lengths, prompt_latent[0], prompt_rope[0], comp_latent[0, 0], comp_rope[0, 0].T,
        query_nope[0, 0], query_rope[0, 0], grad_out[0, 0], w_uk, w_uv,
    )
    outs = pl.pallas_call(
        finish,
        out_shape=[
            jax.ShapeDtypeStruct((8, DC), F32), jax.ShapeDtypeStruct((8, DR), F32),
            jax.ShapeDtypeStruct((16, 2048), F32), jax.ShapeDtypeStruct((16, 2048), F32),
        ],
        name="outputs",
    )(lat, weights)
    return (outs[0][None], outs[1][None], outs[2], outs[3])


def solution(mesh):
    in_specs = (
        P("dp", ("sample", "head"), None),
        P("dp", ("sample", "head"), None),
        P("dp", "sample", None, None),
        P("dp", "sample", None, None),
        P("dp", "sample", None, "head"),
        P("dp", "sample", None, "head"),
        P("dp", "sample", None, "head"),
        P("dp", "sample"),
        P(None, "head"),
        P(None, "head"),
    )
    out_specs = (
        P("dp", ("sample", "head"), None),
        P("dp", ("sample", "head"), None),
        P(("dp", "sample"), "head"),
        P(("dp", "sample"), "head"),
    )
    return jax.shard_map(local, mesh=mesh, in_specs=in_specs, out_specs=out_specs, check_vma=False)
```

```python
import math

import jax
import jax.numpy as jnp
from jax import lax
from jax.experimental import pallas as pl
from jax.experimental.pallas import tpu as pltpu
from jax.sharding import PartitionSpec as P

DH = 128
DR = 64
DC = 512
PLEN = 512
CLEN = 256
KEYS = PLEN + CLEN
WIDE = 640
ACOLS = 384
BCOLS = WIDE - ACOLS
PACK = 384
PAIRS = 8
NT = (((1,), (1,)), ((), ()))
SCALE = 1.0 / (DH + DR) ** 0.5
F32 = jnp.float32
BF16 = jnp.bfloat16
MESH = pl.DeviceIdType.MESH
OVER_XY = ((0, 0), (2, 0), (0, 1), (0, 3), (2, 1), (2, 3), (0, 2), (2, 2))
OVER_Z = (0, 1, 7, 2, 6, 3, 5, 4)
ALL_XY = tuple((dx, dy) for dx in range(4) for dy in range(4) if dx or dy)


def kernel(
    len_hbm, plat_hbm, prope_hbm, clat_hbm, crope_hbm, q_hbm, qr_hbm, g_hbm, wk_hbm, wv_hbm,
    glat_ref, gw_ref,
    plat, prope, clat, crope, q_ref, qr_ref, g_ref, wk_ref, wv_ref, len_ref,
    gz, lat, lat_t, rsel, kv, dkv, dkv_new, lacc, racc,
    wpart, crecv, csum, drecv, apart, a1recv, a2src, a2recv, bpart, b1recv, b2src, b2recv,
    load, gz_send, gz_recv, gy_send, gy_recv, c_send, c_recv, d_send, d_recv,
    a1_send, a1_recv, a2_send, a2_recv, b1_send, b1_recv, b2_send, b2_recv,
):
    step = pl.program_id(0)
    dp, sample, z = lax.axis_index("dp"), lax.axis_index("sample"), lax.axis_index("head")
    x_lo, core = dp // 2, dp % 2
    y, x_hi = sample // 2, sample % 2
    x = x_hi * 2 + x_lo

    def at_xy(dx, dy):
        to = (x + dx) % 4
        return {"dp": (to % 2) * 2 + core, "sample": ((y + dy) % 4) * 2 + to // 2}

    def at_z(d):
        return {"head": (z + d) % 8}

    other_core = {"dp": x_lo * 2 + 1 - core}

    def remote(src, dst, send, recv, device):
        return pltpu.make_async_remote_copy(
            src_ref=src, dst_ref=dst, send_sem=send, recv_sem=recv, device_id=device, device_id_type=MESH
        )

    def arrived(ref, sem):
        pltpu.make_async_copy(ref, ref, sem).wait()

    def swap_core(i):
        return remote(wpart.at[i, :, 1 - core], crecv.at[i], c_send.at[i], c_recv.at[i], other_core)

    def project(first, count):
        rows = lat[first : first + count, :, :DC].reshape(count * 64, DC)

        def pair(i, carry):
            cols = pl.ds(pl.multiple_of(i * 256, 256), 256)
            for half, w in enumerate((wk_ref, wv_ref)):
                kv[i, half, first * 64 : (first + count) * 64] = jnp.dot(
                    rows, w[:, cols], preferred_element_type=F32
                ).astype(BF16)
            return carry

        lax.fori_loop(0, PAIRS, pair, 0)
        tokens = slice(first * 64, (first + count) * 64)
        lat_t[:, tokens] = rows.T
        rope = lat[first : first + count, :, DC:].reshape(count * 64, DH)
        rsel[0, tokens] = rope
        rsel[1, tokens] = jnp.concatenate([jnp.zeros((count * 64, DR), BF16), rope[:, :DR]], 1)

    @pl.when(step == 0)
    def _():
        pairs = (
            (plat_hbm, plat), (prope_hbm, prope), (clat_hbm, clat), (crope_hbm, crope), (wk_hbm, wk_ref),
            (wv_hbm, wv_ref), (q_hbm, q_ref), (qr_hbm, qr_ref), (g_hbm, g_ref), (len_hbm, len_ref),
        )
        loads = [pltpu.make_async_copy(src, dst, load.at[n]) for n, (src, dst) in enumerate(pairs)]
        for copy in loads:
            copy.start()
        barrier = pltpu.get_barrier_semaphore()
        peers = [other_core] + [at_xy(dx, dy) for dx, dy in ALL_XY] + [at_z(d) for d in range(1, 8)]
        for peer in peers:
            pl.semaphore_signal(barrier, inc=1, device_id=peer, device_id_type=MESH)
        loads[0].wait()
        loads[1].wait()
        wide = jnp.concatenate([plat[...].astype(F32), prope[...].astype(F32), jnp.zeros((8, 2 * PACK - DC - DR), F32)], 1)
        gz[0] = jnp.concatenate([wide[:, :PACK], wide[:, PACK:]], 0).astype(BF16)
        pl.semaphore_wait(barrier, len(peers))
        for k in range(1, 8):
            remote(gz.at[0], gz.at[k], gz_send, gz_recv, at_z(8 - OVER_Z[k])).start()
        loads[2].wait()
        loads[3].wait()
        lat[8:12, :, :DC] = clat[...].reshape(4, 64, DC)
        rope = jnp.concatenate([crope[...].astype(F32).T, jnp.zeros((CLEN, WIDE - DC - DR), F32)], 1)
        lat[8:12, :, DC:] = rope.astype(BF16).reshape(4, 64, WIDE - DC)
        dkv[...] = jnp.zeros_like(dkv)
        lacc[...] = jnp.zeros_like(lacc)
        racc[...] = jnp.zeros_like(racc)
        loads[4].wait()
        loads[5].wait()
        project(8, 4)
        arrived(gz.at[pl.ds(1, 7)], gz_recv)
        block = gz[...].astype(F32)
        lat[0] = jnp.concatenate([block[:, :8], block[:, 8:, : WIDE - PACK]], 2).reshape(64, WIDE).astype(BF16)
        for b in range(1, 8):
            dx, dy = OVER_XY[b]
            remote(lat.at[0], lat.at[b], gy_send, gy_recv.at[b // 4], at_xy(4 - dx, 4 - dy)).start()
        for copy in loads[6:]:
            copy.wait()
        live = lax.broadcasted_iota(jnp.int32, g_ref.shape, 0) < len_ref[...]
        g_ref[...] = jnp.where(live, g_ref[...], jnp.zeros((), BF16))
        arrived(lat.at[pl.ds(1, 3)], gy_recv.at[0])
        project(0, 4)
        arrived(lat.at[pl.ds(4, 4)], gy_recv.at[1])
        project(4, 4)
        arrived(gz.at[pl.ds(1, 7)], gz_send)
        arrived(lat.at[pl.ds(1, 7)], gy_send)

    def weights_of(i):
        part = jnp.dot(lat_t[...], dkv[...], preferred_element_type=F32).astype(BF16)
        wpart[i] = part.reshape(2, 2, 4, 2, 16, 512)

    def latents_of(i):
        cols = pl.ds(pl.multiple_of(i * 256, 256), 256)
        both = jnp.concatenate([wk_ref[:, cols], wv_ref[:, cols]], 1)
        lacc[...] += lax.dot_general(dkv[:PLEN], both, NT, preferred_element_type=F32)

    def add_core(i):
        swap_core(i).wait()
        for lo in range(2):
            csum[i, lo] = (wpart[i, lo, core].astype(F32) + crecv[i, lo].astype(F32)).astype(BF16)
        for n, (dx, dy) in enumerate(ALL_XY):
            to = (x + dx) % 4
            remote(
                csum.at[i, to % 2, (y + dy) % 4, to // 2], drecv.at[i, n], d_send.at[i], d_recv.at[i], at_xy(dx, dy)
            ).start()

    def add_owned(i):
        arrived(drecv.at[i], d_recv.at[i])
        total = csum[i, x_lo, y, x_hi].astype(F32)
        for n in range(15):
            total = total + drecv[i, n].astype(F32)
        cols = pl.ds(pl.multiple_of(i * 256, 256), 256)
        gw_ref[0, :, cols] = total[:, :256]
        gw_ref[1, :, cols] = total[:, 256:]
        arrived(drecv.at[i], d_send.at[i])

    before = jnp.maximum(step - 1, 0)
    pair = pl.ds(pl.multiple_of(step * 256, 256), 256)
    qr = qr_ref[:, pl.ds(pl.multiple_of(step * DH, DH), DH)]
    see = lax.broadcasted_iota(jnp.int32, (CLEN, CLEN), 0) <= lax.broadcasted_iota(jnp.int32, (CLEN, CLEN), 1)
    keys, vals = kv[step, 0], kv[step, 1]
    q, g = q_ref[:, pair], g_ref[:, pair]
    for h in range(2):
        cols = slice(h * DH, (h + 1) * DH)
        kx = jnp.concatenate([keys[:, cols], rsel[h]], 1)
        qx = jnp.concatenate([q[:, cols], qr], 1)
        gh = g[:, cols]
        s = lax.dot_general(kx, qx, NT, preferred_element_type=F32)
        s = jnp.concatenate([s[:PLEN], jnp.where(see, s[PLEN:], -1e30)], 0)
        if h == 0:
            weights_of(before)
        else:
            latents_of(before)
        m = jnp.max(s, axis=0, keepdims=True)
        p = jnp.exp2((s - m) * (SCALE * math.log2(math.e)))
        p = p * (1.0 / jnp.sum(p, axis=0, keepdims=True))
        pb = p.astype(BF16)
        dprob = lax.dot_general(vals[:, cols], gh, NT, preferred_element_type=F32)
        delta = jnp.sum(pb.astype(F32) * dprob, axis=0, keepdims=True)
        ds = (p * (dprob - delta)).astype(BF16)
        dk = jnp.dot(ds, qx, preferred_element_type=F32)
        dkv_new[:, cols] = (dk[:, :DH] * SCALE).astype(BF16)
        racc[h] += dk[:PLEN, DH:]
        dkv_new[:, 256 + h * DH : 256 + (h + 1) * DH] = jnp.dot(pb, gh, preferred_element_type=F32).astype(BF16)
    dkv[...] = dkv_new[...]

    @pl.when(step >= 1)
    def _():
        swap_core(step - 1).start()

    @pl.when((step >= 2) & (step < PAIRS - 1))
    def _():
        add_core(step - 2)

    @pl.when((step >= 3) & (step < PAIRS - 1))
    def _():
        add_owned(step - 3)

    @pl.when(step == PAIRS - 1)
    def _():
        last = PAIRS - 1
        latents_of(last)
        apart[...] = lacc[:, :ACOLS].astype(BF16).reshape(8, 64, ACOLS)
        for b in range(1, 8):
            remote(apart.at[b], a1recv.at[b - 1], a1_send, a1_recv, at_xy(*OVER_XY[b])).start()
        rope = (racc[0, :, :DR] + racc[1, :, DR:]) * SCALE
        rest = jnp.concatenate([lacc[:, ACOLS:], rope, jnp.zeros((PLEN, DH - DR), F32)], 1)
        for k in range(8):
            rows = jnp.concatenate([rest[b * 64 + k * 8 : b * 64 + k * 8 + 8] for b in range(8)], 0)
            bpart[k] = rows.astype(BF16)
        for k in range(1, 8):
            remote(bpart.at[k], b1recv.at[k - 1], b1_send, b1_recv, at_z(OVER_Z[k])).start()
        add_core(last - 2)
        weights_of(last)
        swap_core(last).start()
        add_core(last - 1)
        add_owned(last - 3)
        add_core(last)
        add_owned(last - 2)
        arrived(a1recv, a1_recv)
        total = apart[0].astype(F32)
        for b in range(7):
            total = total + a1recv[b].astype(F32)
        a2src[...] = total.reshape(8, 8, ACOLS)
        for k in range(1, 8):
            remote(a2src.at[k], a2recv.at[k - 1], a2_send, a2_recv, at_z(OVER_Z[k])).start()
        arrived(b1recv, b1_recv)
        total = bpart[0].astype(F32)
        for k in range(7):
            total = total + b1recv[k].astype(F32)
        b2src[...] = total.reshape(8, 8, BCOLS)
        for b in range(1, 8):
            remote(b2src.at[b], b2recv.at[b - 1], b2_send, b2_recv, at_xy(*OVER_XY[b])).start()
        add_owned(last - 1)
        add_owned(last)
        arrived(a2recv, a2_recv)
        total = a2src[0]
        for k in range(7):
            total = total + a2recv[k]
        glat_ref[:, :ACOLS] = total
        arrived(b2recv, b2_recv)
        total = b2src[0]
        for b in range(7):
            total = total + b2recv[b]
        glat_ref[:, ACOLS:] = total
        arrived(a1recv, a1_send)
        arrived(b1recv, b1_send)
        arrived(a2recv, a2_send)
        arrived(b2recv, b2_send)


def finish(lat_ref, w_ref, glat_ref, grope_ref, gwk_ref, gwv_ref):
    glat_ref[...] = lat_ref[:, :DC]
    grope_ref[...] = lat_ref[:, DC : DC + DR]
    gwk_ref[...] = w_ref[0]
    gwv_ref[...] = w_ref[1]


def local(prompt_latent, prompt_rope, comp_latent, comp_rope, query_nope, query_rope, grad_out, lengths, w_uk, w_uv):
    def whole(*shape):
        return pl.BlockSpec(shape, lambda i: (0,) * len(shape))

    vmem, dma = pltpu.VMEM, pltpu.SemaphoreType.DMA
    lat, weights = pl.pallas_call(
        kernel,
        grid=(PAIRS,),
        in_specs=[pl.BlockSpec(memory_space=pl.ANY)] * 10,
        out_specs=[whole(8, WIDE), whole(2, 16, 2048)],
        out_shape=[jax.ShapeDtypeStruct((8, WIDE), F32), jax.ShapeDtypeStruct((2, 16, 2048), F32)],
        scratch_shapes=[
            vmem((8, DC), BF16), vmem((8, DR), BF16), vmem((CLEN, DC), BF16), vmem((DR, CLEN), BF16),
            vmem((CLEN, 2048), BF16), vmem((CLEN, 1024), BF16), vmem((CLEN, 2048), BF16),
            vmem((DC, 2048), BF16), vmem((DC, 2048), BF16), vmem((1, 1), jnp.int32),
            vmem((8, 16, PACK), BF16), vmem((12, 64, WIDE), BF16), vmem((DC, KEYS), BF16), vmem((2, KEYS, DH), BF16),
            vmem((PAIRS, 2, KEYS, 256), BF16), vmem((KEYS, 512), BF16), vmem((KEYS, 512), BF16),
            vmem((PLEN, DC), F32), vmem((2, PLEN, DH), F32),
            vmem((PAIRS, 2, 2, 4, 2, 16, 512), BF16),
            vmem((PAIRS, 2, 4, 2, 16, 512), BF16), vmem((PAIRS, 2, 4, 2, 16, 512), BF16),
            vmem((PAIRS, 15, 16, 512), BF16),
            vmem((8, 64, ACOLS), BF16), vmem((7, 64, ACOLS), BF16), vmem((8, 8, ACOLS), F32), vmem((7, 8, ACOLS), F32),
            vmem((8, 64, BCOLS), BF16), vmem((7, 64, BCOLS), BF16), vmem((8, 8, BCOLS), F32), vmem((7, 8, BCOLS), F32),
            dma((10,)), dma, dma, dma, dma((2,)), dma((PAIRS,)), dma((PAIRS,)), dma((PAIRS,)), dma((PAIRS,)),
            dma, dma, dma, dma, dma, dma, dma, dma,
        ],
        compiler_params=pltpu.CompilerParams(
            vmem_limit_bytes=56 * 1024 * 1024, collective_id=0, has_side_effects=True
        ),
        cost_estimate=pl.CostEstimate(flops=13_000_000_000, bytes_accessed=8_000_000, transcendentals=3_200_000),
        name="mla_backward",
    )(
        lengths, prompt_latent[0], prompt_rope[0], comp_latent[0, 0], comp_rope[0, 0].T,
        query_nope[0, 0], query_rope[0, 0], grad_out[0, 0], w_uk, w_uv,
    )
    outs = pl.pallas_call(
        finish,
        out_shape=[
            jax.ShapeDtypeStruct((8, DC), F32), jax.ShapeDtypeStruct((8, DR), F32),
            jax.ShapeDtypeStruct((16, 2048), F32), jax.ShapeDtypeStruct((16, 2048), F32),
        ],
        name="outputs",
    )(lat, weights)
    return (outs[0][None], outs[1][None], outs[2], outs[3])


def solution(mesh):
    in_specs = (
        P("dp", ("sample", "head"), None),
        P("dp", ("sample", "head"), None),
        P("dp", "sample", None, None),
        P("dp", "sample", None, None),
        P("dp", "sample", None, "head"),
        P("dp", "sample", None, "head"),
        P("dp", "sample", None, "head"),
        P("dp", "sample"),
        P(None, "head"),
        P(None, "head"),
    )
    out_specs = (
        P("dp", ("sample", "head"), None),
        P("dp", ("sample", "head"), None),
        P(("dp", "sample"), "head"),
        P(("dp", "sample"), "head"),
    )
    return jax.shard_map(local, mesh=mesh, in_specs=in_specs, out_specs=out_specs, check_vma=False)
```

```python
import math

import jax
import jax.numpy as jnp
from jax import lax
from jax.experimental import pallas as pl
from jax.experimental.pallas import tpu as pltpu
from jax.sharding import PartitionSpec as P

DH = 128
DR = 64
DC = 512
PLEN = 512
CLEN = 256
KEYS = PLEN + CLEN
WIDE = 640
ACOLS = 384
BCOLS = WIDE - ACOLS
PACK = 384
PAIRS = 8
LAG = 5
NT = (((1,), (1,)), ((), ()))
SCALE = 1.0 / (DH + DR) ** 0.5
F32 = jnp.float32
BF16 = jnp.bfloat16
MESH = pl.DeviceIdType.MESH
OVER_XY = ((0, 0), (2, 0), (0, 1), (0, 3), (2, 1), (2, 3), (0, 2), (2, 2))
OVER_Z = (0, 1, 7, 2, 6, 3, 5, 4)
ALL_XY = tuple((dx, dy) for dx in range(4) for dy in range(4) if dx or dy)


def kernel(
    len_hbm, plat_hbm, prope_hbm, clat_hbm, crope_hbm, q_hbm, qr_hbm, g_hbm, wk_hbm, wv_hbm,
    glat_ref, gw_ref,
    plat, prope, clat, crope, q_ref, qr_ref, g_ref, wk_ref, wv_ref, len_ref,
    gz, lat, lat_t, rsel, kv, dkv, dkv_new, lacc, racc,
    wpart, crecv, csum, drecv, apart, a1recv, a2src, a2recv, bpart, b1recv, b2src, b2recv,
    load, gz_send, gz_recv, gy_send, gy_recv, c_send, c_recv, d_send, d_recv,
    a1_send, a1_recv, a2_send, a2_recv, b1_send, b1_recv, b2_send, b2_recv,
):
    step = pl.program_id(0)
    dp, sample, z = lax.axis_index("dp"), lax.axis_index("sample"), lax.axis_index("head")
    x_lo, core = dp // 2, dp % 2
    y, x_hi = sample // 2, sample % 2
    x = x_hi * 2 + x_lo

    def at_xy(dx, dy):
        to = (x + dx) % 4
        return {"dp": (to % 2) * 2 + core, "sample": ((y + dy) % 4) * 2 + to // 2}

    def at_z(d):
        return {"head": (z + d) % 8}

    other_core = {"dp": x_lo * 2 + 1 - core}

    def remote(src, dst, send, recv, device):
        return pltpu.make_async_remote_copy(
            src_ref=src, dst_ref=dst, send_sem=send, recv_sem=recv, device_id=device, device_id_type=MESH
        )

    def arrived(ref, sem):
        pltpu.make_async_copy(ref, ref, sem).wait()

    def swap_core(i):
        return remote(wpart.at[i, :, 1 - core], crecv.at[i], c_send.at[i], c_recv.at[i], other_core)

    def project(first, count):
        rows = lat[first : first + count, :, :DC].reshape(count * 64, DC)

        for i in range(PAIRS):
            cols = slice(i * 256, (i + 1) * 256)
            for half, w in enumerate((wk_ref, wv_ref)):
                kv[i, half, first * 64 : (first + count) * 64] = jnp.dot(
                    rows, w[:, cols], preferred_element_type=F32
                ).astype(BF16)
        tokens = slice(first * 64, (first + count) * 64)
        lat_t[:, tokens] = rows.T
        rope = lat[first : first + count, :, DC:].reshape(count * 64, DH)
        rsel[0, tokens] = rope
        rsel[1, tokens] = jnp.concatenate([jnp.zeros((count * 64, DR), BF16), rope[:, :DR]], 1)

    @pl.when(step == 0)
    def _():
        pairs = (
            (plat_hbm, plat), (prope_hbm, prope), (clat_hbm, clat), (crope_hbm, crope), (wk_hbm, wk_ref),
            (wv_hbm, wv_ref), (q_hbm, q_ref), (qr_hbm, qr_ref), (g_hbm, g_ref), (len_hbm, len_ref),
        )
        loads = [pltpu.make_async_copy(src, dst, load.at[n]) for n, (src, dst) in enumerate(pairs)]
        for copy in loads:
            copy.start()
        barrier = pltpu.get_barrier_semaphore()
        peers = [other_core] + [at_xy(dx, dy) for dx, dy in ALL_XY] + [at_z(d) for d in range(1, 8)]
        for peer in peers:
            pl.semaphore_signal(barrier, inc=1, device_id=peer, device_id_type=MESH)
        loads[0].wait()
        loads[1].wait()
        wide = jnp.concatenate([plat[...].astype(F32), prope[...].astype(F32), jnp.zeros((8, 2 * PACK - DC - DR), F32)], 1)
        gz[0] = jnp.concatenate([wide[:, :PACK], wide[:, PACK:]], 0).astype(BF16)
        pl.semaphore_wait(barrier, len(peers))
        for k in range(1, 8):
            remote(gz.at[0], gz.at[k], gz_send, gz_recv, at_z(8 - OVER_Z[k])).start()
        loads[2].wait()
        loads[3].wait()
        lat[8:12, :, :DC] = clat[...].reshape(4, 64, DC)
        rope = jnp.concatenate([crope[...].astype(F32).T, jnp.zeros((CLEN, WIDE - DC - DR), F32)], 1)
        lat[8:12, :, DC:] = rope.astype(BF16).reshape(4, 64, WIDE - DC)
        dkv[...] = jnp.zeros_like(dkv)
        lacc[...] = jnp.zeros_like(lacc)
        racc[...] = jnp.zeros_like(racc)
        loads[4].wait()
        loads[5].wait()
        project(8, 4)
        arrived(gz.at[pl.ds(1, 7)], gz_recv)
        block = gz[...].astype(F32)
        lat[0] = jnp.concatenate([block[:, :8], block[:, 8:, : WIDE - PACK]], 2).reshape(64, WIDE).astype(BF16)
        for b in range(1, 8):
            dx, dy = OVER_XY[b]
            remote(lat.at[0], lat.at[b], gy_send, gy_recv.at[b // 4], at_xy(4 - dx, 4 - dy)).start()
        for copy in loads[6:]:
            copy.wait()
        live = lax.broadcasted_iota(jnp.int32, g_ref.shape, 0) < len_ref[...]
        g_ref[...] = jnp.where(live, g_ref[...], jnp.zeros((), BF16))
        arrived(lat.at[pl.ds(1, 3)], gy_recv.at[0])
        project(0, 4)
        arrived(lat.at[pl.ds(4, 4)], gy_recv.at[1])
        project(4, 4)
        arrived(gz.at[pl.ds(1, 7)], gz_send)
        arrived(lat.at[pl.ds(1, 7)], gy_send)

    def weights_of(i):
        part = jnp.dot(lat_t[...], dkv[...], preferred_element_type=F32).astype(BF16)
        wpart[i] = part.reshape(2, 2, 4, 2, 16, 512)

    def latents_of(i):
        cols = pl.ds(pl.multiple_of(i * 256, 256), 256)
        both = jnp.concatenate([wk_ref[:, cols], wv_ref[:, cols]], 1)
        lacc[...] += lax.dot_general(dkv[:PLEN], both, NT, preferred_element_type=F32)

    def add_core(i):
        swap_core(i).wait()
        for lo in range(2):
            csum[i, lo] = (wpart[i, lo, core].astype(F32) + crecv[i, lo].astype(F32)).astype(BF16)
        for n, (dx, dy) in enumerate(ALL_XY):
            to = (x + dx) % 4
            remote(
                csum.at[i, to % 2, (y + dy) % 4, to // 2], drecv.at[i, n], d_send.at[i], d_recv.at[i], at_xy(dx, dy)
            ).start()

    def add_owned(i):
        arrived(drecv.at[i], d_recv.at[i])
        total = csum[i, x_lo, y, x_hi].astype(F32)
        for n in range(15):
            total = total + drecv[i, n].astype(F32)
        cols = pl.ds(pl.multiple_of(i * 256, 256), 256)
        gw_ref[0, :, cols] = total[:, :256]
        gw_ref[1, :, cols] = total[:, 256:]
        arrived(drecv.at[i], d_send.at[i])

    before = jnp.maximum(step - 1, 0)
    pair = pl.ds(pl.multiple_of(step * 256, 256), 256)
    qr = qr_ref[:, pl.ds(pl.multiple_of(step * DH, DH), DH)]
    see = lax.broadcasted_iota(jnp.int32, (CLEN, CLEN), 0) <= lax.broadcasted_iota(jnp.int32, (CLEN, CLEN), 1)
    keys, vals = kv[step, 0], kv[step, 1]
    q, g = q_ref[:, pair], g_ref[:, pair]
    for h in range(2):
        cols = slice(h * DH, (h + 1) * DH)
        kx = jnp.concatenate([keys[:, cols], rsel[h]], 1)
        qx = jnp.concatenate([q[:, cols], qr], 1)
        gh = g[:, cols]
        s = lax.dot_general(kx, qx, NT, preferred_element_type=F32)
        s = jnp.concatenate([s[:PLEN], jnp.where(see, s[PLEN:], -1e30)], 0)
        if h == 0:
            weights_of(before)
        else:
            latents_of(before)
        m = jnp.max(s, axis=0, keepdims=True)
        p = jnp.exp2((s - m) * (SCALE * math.log2(math.e)))
        p = p * (1.0 / jnp.sum(p, axis=0, keepdims=True))
        pb = p.astype(BF16)
        dprob = lax.dot_general(vals[:, cols], gh, NT, preferred_element_type=F32)
        delta = jnp.sum(pb.astype(F32) * dprob, axis=0, keepdims=True)
        ds = (p * (dprob - delta)).astype(BF16)
        dk = jnp.dot(ds, qx, preferred_element_type=F32)
        dkv_new[:, cols] = (dk[:, :DH] * SCALE).astype(BF16)
        racc[h] += dk[:PLEN, DH:]
        dkv_new[:, 256 + h * DH : 256 + (h + 1) * DH] = jnp.dot(pb, gh, preferred_element_type=F32).astype(BF16)
    dkv[...] = dkv_new[...]

    @pl.when(step >= 1)
    def _():
        swap_core(step - 1).start()

    @pl.when((step >= 2) & (step < PAIRS - 1))
    def _():
        add_core(step - 2)

    @pl.when((step >= LAG) & (step < PAIRS - 1))
    def _():
        add_owned(step - LAG)

    @pl.when(step == PAIRS - 1)
    def _():
        last = PAIRS - 1
        latents_of(last)
        apart[...] = lacc[:, :ACOLS].astype(BF16).reshape(8, 64, ACOLS)
        for b in range(1, 8):
            remote(apart.at[b], a1recv.at[b - 1], a1_send, a1_recv, at_xy(*OVER_XY[b])).start()
        rope = (racc[0, :, :DR] + racc[1, :, DR:]) * SCALE
        rest = jnp.concatenate([lacc[:, ACOLS:], rope, jnp.zeros((PLEN, DH - DR), F32)], 1)
        for k in range(8):
            rows = jnp.concatenate([rest[b * 64 + k * 8 : b * 64 + k * 8 + 8] for b in range(8)], 0)
            bpart[k] = rows.astype(BF16)
        for k in range(1, 8):
            remote(bpart.at[k], b1recv.at[k - 1], b1_send, b1_recv, at_z(OVER_Z[k])).start()
        add_core(last - 2)
        weights_of(last)
        swap_core(last).start()
        add_core(last - 1)
        for i in range(last - LAG, last - 3):
            add_owned(i)
        add_core(last)
        add_owned(last - 3)
        arrived(a1recv, a1_recv)
        total = apart[0].astype(F32)
        for b in range(7):
            total = total + a1recv[b].astype(F32)
        a2src[...] = total.reshape(8, 8, ACOLS)
        for k in range(1, 8):
            remote(a2src.at[k], a2recv.at[k - 1], a2_send, a2_recv, at_z(OVER_Z[k])).start()
        arrived(b1recv, b1_recv)
        total = bpart[0].astype(F32)
        for k in range(7):
            total = total + b1recv[k].astype(F32)
        b2src[...] = total.reshape(8, 8, BCOLS)
        for b in range(1, 8):
            remote(b2src.at[b], b2recv.at[b - 1], b2_send, b2_recv, at_xy(*OVER_XY[b])).start()
        for i in range(last - 2, last + 1):
            add_owned(i)
        arrived(a2recv, a2_recv)
        total = a2src[0]
        for k in range(7):
            total = total + a2recv[k]
        glat_ref[:, :ACOLS] = total
        arrived(b2recv, b2_recv)
        total = b2src[0]
        for b in range(7):
            total = total + b2recv[b]
        glat_ref[:, ACOLS:] = total
        arrived(a1recv, a1_send)
        arrived(b1recv, b1_send)
        arrived(a2recv, a2_send)
        arrived(b2recv, b2_send)


def finish(lat_ref, w_ref, glat_ref, grope_ref, gwk_ref, gwv_ref):
    glat_ref[...] = lat_ref[:, :DC]
    grope_ref[...] = lat_ref[:, DC : DC + DR]
    gwk_ref[...] = w_ref[0]
    gwv_ref[...] = w_ref[1]


def local(prompt_latent, prompt_rope, comp_latent, comp_rope, query_nope, query_rope, grad_out, lengths, w_uk, w_uv):
    def whole(*shape):
        return pl.BlockSpec(shape, lambda i: (0,) * len(shape))

    vmem, dma = pltpu.VMEM, pltpu.SemaphoreType.DMA
    lat, weights = pl.pallas_call(
        kernel,
        grid=(PAIRS,),
        in_specs=[pl.BlockSpec(memory_space=pl.ANY)] * 10,
        out_specs=[whole(8, WIDE), whole(2, 16, 2048)],
        out_shape=[jax.ShapeDtypeStruct((8, WIDE), F32), jax.ShapeDtypeStruct((2, 16, 2048), F32)],
        scratch_shapes=[
            vmem((8, DC), BF16), vmem((8, DR), BF16), vmem((CLEN, DC), BF16), vmem((DR, CLEN), BF16),
            vmem((CLEN, 2048), BF16), vmem((CLEN, 1024), BF16), vmem((CLEN, 2048), BF16),
            vmem((DC, 2048), BF16), vmem((DC, 2048), BF16), vmem((1, 1), jnp.int32),
            vmem((8, 16, PACK), BF16), vmem((12, 64, WIDE), BF16), vmem((DC, KEYS), BF16), vmem((2, KEYS, DH), BF16),
            vmem((PAIRS, 2, KEYS, 256), BF16), vmem((KEYS, 512), BF16), vmem((KEYS, 512), BF16),
            vmem((PLEN, DC), F32), vmem((2, PLEN, DH), F32),
            vmem((PAIRS, 2, 2, 4, 2, 16, 512), BF16),
            vmem((PAIRS, 2, 4, 2, 16, 512), BF16), vmem((PAIRS, 2, 4, 2, 16, 512), BF16),
            vmem((PAIRS, 15, 16, 512), BF16),
            vmem((8, 64, ACOLS), BF16), vmem((7, 64, ACOLS), BF16), vmem((8, 8, ACOLS), F32), vmem((7, 8, ACOLS), F32),
            vmem((8, 64, BCOLS), BF16), vmem((7, 64, BCOLS), BF16), vmem((8, 8, BCOLS), F32), vmem((7, 8, BCOLS), F32),
            dma((10,)), dma, dma, dma, dma((2,)), dma((PAIRS,)), dma((PAIRS,)), dma((PAIRS,)), dma((PAIRS,)),
            dma, dma, dma, dma, dma, dma, dma, dma,
        ],
        compiler_params=pltpu.CompilerParams(
            vmem_limit_bytes=56 * 1024 * 1024, collective_id=0, has_side_effects=True
        ),
        cost_estimate=pl.CostEstimate(flops=13_000_000_000, bytes_accessed=8_000_000, transcendentals=3_200_000),
        name="mla_backward",
    )(
        lengths, prompt_latent[0], prompt_rope[0], comp_latent[0, 0], comp_rope[0, 0].T,
        query_nope[0, 0], query_rope[0, 0], grad_out[0, 0], w_uk, w_uv,
    )
    outs = pl.pallas_call(
        finish,
        out_shape=[
            jax.ShapeDtypeStruct((8, DC), F32), jax.ShapeDtypeStruct((8, DR), F32),
            jax.ShapeDtypeStruct((16, 2048), F32), jax.ShapeDtypeStruct((16, 2048), F32),
        ],
        name="outputs",
    )(lat, weights)
    return (outs[0][None], outs[1][None], outs[2], outs[3])


def solution(mesh):
    in_specs = (
        P("dp", ("sample", "head"), None),
        P("dp", ("sample", "head"), None),
        P("dp", "sample", None, None),
        P("dp", "sample", None, None),
        P("dp", "sample", None, "head"),
        P("dp", "sample", None, "head"),
        P("dp", "sample", None, "head"),
        P("dp", "sample"),
        P(None, "head"),
        P(None, "head"),
    )
    out_specs = (
        P("dp", ("sample", "head"), None),
        P("dp", ("sample", "head"), None),
        P(("dp", "sample"), "head"),
        P(("dp", "sample"), "head"),
    )
    return jax.shard_map(local, mesh=mesh, in_specs=in_specs, out_specs=out_specs, check_vma=False)
```

```python
import math

import jax
import jax.numpy as jnp
from jax import lax
from jax.experimental import pallas as pl
from jax.experimental.pallas import tpu as pltpu
from jax.sharding import PartitionSpec as P

DH = 128
DR = 64
DC = 512
PLEN = 512
CLEN = 256
KEYS = PLEN + CLEN
WIDE = 640
ACOLS = 384
BCOLS = WIDE - ACOLS
PACK = 384
PAIRS = 8
STEPS = PAIRS // 2
NT = (((1,), (1,)), ((), ()))
SCALE = 1.0 / (DH + DR) ** 0.5
F32 = jnp.float32
BF16 = jnp.bfloat16
MESH = pl.DeviceIdType.MESH
OVER_XY = ((0, 0), (2, 0), (0, 1), (0, 3), (2, 1), (2, 3), (0, 2), (2, 2))
OVER_Z = (0, 1, 7, 2, 6, 3, 5, 4)
ALL_XY = tuple((dx, dy) for dx in range(4) for dy in range(4) if dx or dy)


def kernel(
    len_hbm, plat_hbm, prope_hbm, clat_hbm, crope_hbm, q_hbm, qr_hbm, g_hbm, wk_hbm, wv_hbm,
    glat_ref, gw_ref,
    plat, prope, clat, crope, q_ref, qr_ref, g_ref, wk_ref, wv_ref, len_ref,
    gz, gl, gr, lat, lat_t, rsel, kv, dkv_a, dkv_b, lacc, racc,
    wpart, crecv, csum, krecv1, ksum, krecv2, vrecv1, vsum, vrecv2, apart, a1recv, a2src, a2recv, bpart, b1recv, b2src, b2recv,
    load, gz_send, gz_recv, gl_send, gl_recv, gr_send, gr_recv, c_send, c_recv,
    k1_send, k1_recv, k2_send, k2_recv, v1_send, v1_recv, v2_send, v2_recv,
    a1_send, a1_recv, a2_send, a2_recv, b1_send, b1_recv, b2_send, b2_recv,
):
    step = pl.program_id(0)
    dp, sample, z = lax.axis_index("dp"), lax.axis_index("sample"), lax.axis_index("head")
    x_lo, core = dp // 2, dp % 2
    y, x_hi = sample // 2, sample % 2
    x = x_hi * 2 + x_lo

    def at_xy(dx, dy):
        to = (x + dx) % 4
        return {"dp": (to % 2) * 2 + core, "sample": ((y + dy) % 4) * 2 + to // 2}

    def at_z(d):
        return {"head": (z + d) % 8}

    other_core = {"dp": x_lo * 2 + 1 - core}

    def remote(src, dst, send, recv, device):
        return pltpu.make_async_remote_copy(
            src_ref=src, dst_ref=dst, send_sem=send, recv_sem=recv, device_id=device, device_id_type=MESH
        )

    def arrived(ref, sem):
        pltpu.make_async_copy(ref, ref, sem).wait()

    def swap_core(i):
        return remote(wpart.at[i, :, 1 - core], crecv.at[i], c_send.at[i], c_recv.at[i], other_core)

    def project(first, count):
        rows = lat[first : first + count, :, :DC].reshape(count * 64, DC)

        for i in range(PAIRS):
            cols = slice(i * 256, (i + 1) * 256)
            for half, w in enumerate((wk_ref, wv_ref)):
                kv[i, half, first * 64 : (first + count) * 64] = jnp.dot(
                    rows, w[:, cols], preferred_element_type=F32
                ).astype(BF16)
        tokens = slice(first * 64, (first + count) * 64)
        lat_t[:, tokens] = rows.T
        rope = lat[first : first + count, :, DC:].reshape(count * 64, DH)
        rsel[0, tokens] = rope
        rsel[1, tokens] = jnp.concatenate([jnp.zeros((count * 64, DR), BF16), rope[:, :DR]], 1)

    @pl.when(step == 0)
    def _():
        pairs = (
            (plat_hbm, plat), (prope_hbm, prope), (clat_hbm, clat), (crope_hbm, crope), (wk_hbm, wk_ref),
            (wv_hbm, wv_ref), (q_hbm, q_ref), (qr_hbm, qr_ref), (g_hbm, g_ref), (len_hbm, len_ref),
        )
        loads = [pltpu.make_async_copy(src, dst, load.at[n]) for n, (src, dst) in enumerate(pairs)]
        for copy in loads:
            copy.start()
        barrier = pltpu.get_barrier_semaphore()
        peers = [other_core] + [at_xy(dx, dy) for dx, dy in ALL_XY] + [at_z(d) for d in range(1, 8)]
        for peer in peers:
            pl.semaphore_signal(barrier, inc=1, device_id=peer, device_id_type=MESH)
        loads[0].wait()
        loads[1].wait()
        wide = plat[...].astype(F32)
        rope = jnp.concatenate([prope[...].astype(F32), jnp.zeros((8, DH - DR), F32)], 1)
        gz[0] = jnp.concatenate(
            [jnp.concatenate([wide[:, :256], wide[:, 256:]], 0), jnp.concatenate([rope, jnp.zeros((8, DH), F32)], 0)], 1
        ).astype(BF16)
        pl.semaphore_wait(barrier, len(peers))
        for k in range(1, 8):
            remote(gz.at[0], gz.at[k], gz_send, gz_recv.at[k // 5], at_z(8 - OVER_Z[k])).start()

        def forward(first, count):
            for b in range(1, 8):
                dx, dy = OVER_XY[b]
                blocks = pl.ds(first, count)
                remote(
                    gz.at[blocks, :, pl.ds(0, 256)], gl.at[b, blocks], gl_send, gl_recv.at[b // 4], at_xy(4 - dx, 4 - dy)
                ).start()

        def unpack(first, count):
            block = gl[first : first + count].astype(F32)
            block = jnp.concatenate([block[:, :, :8], block[:, :, 8:]], 3)
            lat[first : first + count, :, :DC] = block.reshape(count, 64, DC).astype(BF16)
            for b in range(first, first + count):
                rope = gr[b].astype(F32)
                rope = jnp.concatenate([rope[:, :DR], rope[:, DR:]], 0)
                lat[b, :, DC:] = jnp.concatenate([rope, jnp.zeros((64, DH - DR), F32)], 1).astype(BF16)

        forward(0, 1)
        loads[2].wait()
        loads[3].wait()
        lat[8:12, :, :DC] = clat[...].reshape(4, 64, DC)
        rope = jnp.concatenate([crope[...].astype(F32).T, jnp.zeros((CLEN, WIDE - DC - DR), F32)], 1)
        lat[8:12, :, DC:] = rope.astype(BF16).reshape(4, 64, WIDE - DC)
        loads[4].wait()
        loads[5].wait()
        project(8, 4)
        arrived(gz.at[pl.ds(1, 4)], gz_recv.at[0])
        forward(1, 4)
        dkv_b[...] = jnp.zeros_like(dkv_b)
        lacc[...] = jnp.zeros_like(lacc)
        racc[...] = jnp.zeros_like(racc)
        arrived(gz.at[pl.ds(5, 3)], gz_recv.at[1])
        forward(5, 3)
        rope = gz[:, :, 256:].astype(F32)[:, :8, :DR].reshape(64, DR)
        gr[0] = jnp.concatenate([rope[:32], rope[32:]], 1).astype(BF16)
        for b in range(1, 8):
            dx, dy = OVER_XY[b]
            remote(gr.at[0], gr.at[b], gr_send, gr_recv.at[b // 4], at_xy(4 - dx, 4 - dy)).start()
        gl[0] = gz[:, :, :256]
        for copy in loads[6:]:
            copy.wait()
        live = lax.broadcasted_iota(jnp.int32, g_ref.shape, 0) < len_ref[...]
        g_ref[...] = jnp.where(live, g_ref[...], jnp.zeros((), BF16))
        arrived(gl.at[pl.ds(1, 3)], gl_recv.at[0])
        arrived(gr.at[pl.ds(1, 3)], gr_recv.at[0])
        unpack(0, 4)
        project(0, 4)
        arrived(gl.at[pl.ds(4, 4)], gl_recv.at[1])
        arrived(gr.at[pl.ds(4, 4)], gr_recv.at[1])
        unpack(4, 4)
        project(4, 4)
        arrived(gz.at[pl.ds(1, 7)], gz_send)
        arrived(gl.at[pl.ds(1, 7)], gl_send)
        arrived(gr.at[pl.ds(1, 7)], gr_send)

    def weights_of(i, dkv):
        part = jnp.dot(lat_t[...], dkv[...], preferred_element_type=F32).astype(BF16)
        wpart[i] = part.reshape(2, 2, 4, 2, 16, 512)

    def latents_of(i, dkv):
        cols = pl.ds(pl.multiple_of(i * 256, 256), 256)
        both = jnp.concatenate([wk_ref[:, cols], wv_ref[:, cols]], 1)
        lacc[...] += lax.dot_general(dkv[:PLEN], both, NT, preferred_element_type=F32)

    def add_core(i):
        swap_core(i).wait()
        for lo in range(2):
            total = wpart[i, lo, core].astype(F32) + crecv[i, lo].astype(F32)
            csum[i, 0, lo] = total[..., :256].astype(BF16)
            csum[i, 1, lo] = total[..., 256:].astype(BF16)
        for d in (1, 2, 3):
            to = (x + d) % 4
            remote(csum.at[i, 0, to % 2, :, to // 2], krecv1.at[i, d - 1], k1_send.at[i], k1_recv.at[i], at_xy(d, 0)).start()
            remote(csum.at[i, 1, :, (y + d) % 4], vrecv1.at[i, d - 1], v1_send.at[i], v1_recv.at[i], at_xy(0, d)).start()

    def add_first(i):
        arrived(krecv1.at[i], k1_recv.at[i])
        arrived(vrecv1.at[i], v1_recv.at[i])
        k = csum[i, 0, x_lo, :, x_hi].astype(F32)
        v = csum[i, 1, :, y].astype(F32)
        for d in range(3):
            k = k + krecv1[i, d].astype(F32)
            v = v + vrecv1[i, d].astype(F32)
        ksum[i] = k.astype(BF16)
        vsum[i] = v.astype(BF16)
        for d in (1, 2, 3):
            to = (x + d) % 4
            remote(ksum.at[i, (y + d) % 4], krecv2.at[i, d - 1], k2_send.at[i], k2_recv.at[i], at_xy(0, d)).start()
            remote(vsum.at[i, to % 2, to // 2], vrecv2.at[i, d - 1], v2_send.at[i], v2_recv.at[i], at_xy(d, 0)).start()

    def add_owned(i):
        arrived(krecv2.at[i], k2_recv.at[i])
        arrived(vrecv2.at[i], v2_recv.at[i])
        k = ksum[i, y].astype(F32)
        v = vsum[i, x_lo, x_hi].astype(F32)
        for d in range(3):
            k = k + krecv2[i, d].astype(F32)
            v = v + vrecv2[i, d].astype(F32)
        cols = pl.ds(pl.multiple_of(i * 256, 256), 256)
        gw_ref[0, :, cols] = k
        gw_ref[1, :, cols] = v
        arrived(krecv1.at[i], k1_send.at[i])
        arrived(vrecv1.at[i], v1_send.at[i])
        arrived(krecv2.at[i], k2_send.at[i])
        arrived(vrecv2.at[i], v2_send.at[i])

    see = lax.broadcasted_iota(jnp.int32, (CLEN, CLEN), 0) <= lax.broadcasted_iota(jnp.int32, (CLEN, CLEN), 1)

    def attend(i, new, before, old):
        pair = pl.ds(pl.multiple_of(i * 256, 256), 256)
        qr = qr_ref[:, pl.ds(pl.multiple_of(i * DH, DH), DH)]
        keys, vals = kv[i, 0], kv[i, 1]
        q, g = q_ref[:, pair], g_ref[:, pair]
        heads = []
        for h in range(2):
            cols = slice(h * DH, (h + 1) * DH)
            kx = jnp.concatenate([keys[:, cols], rsel[h]], 1)
            qx = jnp.concatenate([q[:, cols], qr], 1)
            s = lax.dot_general(kx, qx, NT, preferred_element_type=F32)
            dprob = lax.dot_general(vals[:, cols], g[:, cols], NT, preferred_element_type=F32)
            heads.append((cols, qx, g[:, cols], s, dprob))
        weights_of(before, old)
        latents_of(before, old)
        for h, (cols, qx, gh, s, dprob) in enumerate(heads):
            s = jnp.concatenate([s[:PLEN], jnp.where(see, s[PLEN:], -1e30)], 0)
            m = jnp.max(s, axis=0, keepdims=True)
            p = jnp.exp2((s - m) * (SCALE * math.log2(math.e)))
            p = p * (1.0 / jnp.sum(p, axis=0, keepdims=True))
            pb = p.astype(BF16)
            new[:, 256 + h * DH : 256 + (h + 1) * DH] = jnp.dot(pb, gh, preferred_element_type=F32).astype(BF16)
            delta = jnp.sum(pb.astype(F32) * dprob, axis=0, keepdims=True)
            ds = (p * (dprob - delta)).astype(BF16)
            dk = jnp.dot(ds, qx, preferred_element_type=F32)
            new[:, cols] = (dk[:, :DH] * SCALE).astype(BF16)
            racc[h] += dk[:PLEN, DH:]

    first, second = 2 * step, 2 * step + 1
    attend(first, dkv_a, jnp.maximum(first - 1, 0), dkv_b)

    @pl.when(step >= 1)
    def _():
        swap_core(first - 1).start()
        add_core(first - 2)

    @pl.when(step >= 2)
    def _():
        add_first(first - 4)

    @pl.when(step >= 3)
    def _():
        add_owned(first - 6)

    attend(second, dkv_b, first, dkv_a)
    swap_core(first).start()

    @pl.when((step >= 1) & (step < STEPS - 1))
    def _():
        add_core(first - 1)

    @pl.when((step >= 2) & (step < STEPS - 1))
    def _():
        add_first(first - 3)

    @pl.when(step == STEPS - 1)
    def _():
        last = PAIRS - 1
        latents_of(last, dkv_b)
        apart[...] = lacc[:, :ACOLS].astype(BF16).reshape(8, 64, ACOLS)
        for b in range(1, 8):
            remote(apart.at[b], a1recv.at[b - 1], a1_send, a1_recv, at_xy(*OVER_XY[b])).start()
        rope = (racc[0, :, :DR] + racc[1, :, DR:]) * SCALE
        rest = jnp.concatenate([lacc[:, ACOLS:], rope, jnp.zeros((PLEN, DH - DR), F32)], 1)
        for k in range(8):
            rows = jnp.concatenate([rest[b * 64 + k * 8 : b * 64 + k * 8 + 8] for b in range(8)], 0)
            bpart[k] = rows.astype(BF16)
        for k in range(1, 8):
            remote(bpart.at[k], b1recv.at[k - 1], b1_send, b1_recv, at_z(OVER_Z[k])).start()
        add_core(last - 2)
        weights_of(last, dkv_b)
        swap_core(last).start()
        add_first(last - 4)
        add_core(last - 1)
        add_first(last - 3)
        add_core(last)
        add_owned(last - 6)
        add_owned(last - 5)
        add_first(last - 2)
        add_first(last - 1)
        arrived(a1recv, a1_recv)
        total = apart[0].astype(F32)
        for b in range(7):
            total = total + a1recv[b].astype(F32)
        a2src[...] = total.reshape(8, 8, ACOLS)
        for k in range(1, 8):
            remote(a2src.at[k], a2recv.at[k - 1], a2_send, a2_recv, at_z(OVER_Z[k])).start()
        add_first(last)
        arrived(b1recv, b1_recv)
        total = bpart[0].astype(F32)
        for k in range(7):
            total = total + b1recv[k].astype(F32)
        b2src[...] = total.reshape(8, 8, BCOLS)
        for b in range(1, 8):
            remote(b2src.at[b], b2recv.at[b - 1], b2_send, b2_recv, at_xy(*OVER_XY[b])).start()
        for i in range(last - 4, last + 1):
            add_owned(i)
        arrived(a2recv, a2_recv)
        total = a2src[0]
        for k in range(7):
            total = total + a2recv[k]
        glat_ref[:, :ACOLS] = total
        arrived(b2recv, b2_recv)
        total = b2src[0]
        for b in range(7):
            total = total + b2recv[b]
        glat_ref[:, ACOLS:] = total
        arrived(a1recv, a1_send)
        arrived(b1recv, b1_send)
        arrived(a2recv, a2_send)
        arrived(b2recv, b2_send)


def finish(lat_ref, w_ref, glat_ref, grope_ref, gwk_ref, gwv_ref):
    glat_ref[...] = lat_ref[:, :DC]
    grope_ref[...] = lat_ref[:, DC : DC + DR]
    gwk_ref[...] = w_ref[0]
    gwv_ref[...] = w_ref[1]


def local(prompt_latent, prompt_rope, comp_latent, comp_rope, query_nope, query_rope, grad_out, lengths, w_uk, w_uv):
    def whole(*shape):
        return pl.BlockSpec(shape, lambda i: (0,) * len(shape))

    vmem, dma = pltpu.VMEM, pltpu.SemaphoreType.DMA
    lat, weights = pl.pallas_call(
        kernel,
        grid=(STEPS,),
        in_specs=[pl.BlockSpec(memory_space=pl.ANY)] * 10,
        out_specs=[whole(8, WIDE), whole(2, 16, 2048)],
        out_shape=[jax.ShapeDtypeStruct((8, WIDE), F32), jax.ShapeDtypeStruct((2, 16, 2048), F32)],
        scratch_shapes=[
            vmem((8, DC), BF16), vmem((8, DR), BF16), vmem((CLEN, DC), BF16), vmem((DR, CLEN), BF16),
            vmem((CLEN, 2048), BF16), vmem((CLEN, 1024), BF16), vmem((CLEN, 2048), BF16),
            vmem((DC, 2048), BF16), vmem((DC, 2048), BF16), vmem((1, 1), jnp.int32),
            vmem((8, 16, PACK), BF16), vmem((8, 8, 16, 256), BF16), vmem((8, 32, DH), BF16),
            vmem((12, 64, WIDE), BF16), vmem((DC, KEYS), BF16), vmem((2, KEYS, DH), BF16),
            vmem((PAIRS, 2, KEYS, 256), BF16), vmem((KEYS, 512), BF16), vmem((KEYS, 512), BF16),
            vmem((PLEN, DC), F32), vmem((2, PLEN, DH), F32),
            vmem((PAIRS, 2, 2, 4, 2, 16, 512), BF16),
            vmem((PAIRS, 2, 4, 2, 16, 512), BF16),
            vmem((PAIRS, 2, 2, 4, 2, 16, 256), BF16),
            vmem((PAIRS, 3, 4, 16, 256), BF16), vmem((PAIRS, 4, 16, 256), BF16), vmem((PAIRS, 3, 16, 256), BF16),
            vmem((PAIRS, 3, 2, 2, 16, 256), BF16), vmem((PAIRS, 2, 2, 16, 256), BF16), vmem((PAIRS, 3, 16, 256), BF16),
            vmem((8, 64, ACOLS), BF16), vmem((7, 64, ACOLS), BF16), vmem((8, 8, ACOLS), F32), vmem((7, 8, ACOLS), F32),
            vmem((8, 64, BCOLS), BF16), vmem((7, 64, BCOLS), BF16), vmem((8, 8, BCOLS), F32), vmem((7, 8, BCOLS), F32),
            dma((10,)), dma, dma((2,)), dma, dma((2,)), dma, dma((2,)),
            *[dma((PAIRS,))] * 10, *[dma] * 8,
        ],
        compiler_params=pltpu.CompilerParams(
            vmem_limit_bytes=56 * 1024 * 1024, collective_id=0, has_side_effects=True
        ),
        cost_estimate=pl.CostEstimate(flops=13_000_000_000, bytes_accessed=8_000_000, transcendentals=3_200_000),
        name="mla_backward",
    )(
        lengths, prompt_latent[0], prompt_rope[0], comp_latent[0, 0], comp_rope[0, 0].T,
        query_nope[0, 0], query_rope[0, 0], grad_out[0, 0], w_uk, w_uv,
    )
    outs = pl.pallas_call(
        finish,
        out_shape=[
            jax.ShapeDtypeStruct((8, DC), F32), jax.ShapeDtypeStruct((8, DR), F32),
            jax.ShapeDtypeStruct((16, 2048), F32), jax.ShapeDtypeStruct((16, 2048), F32),
        ],
        name="outputs",
    )(lat, weights)
    return (outs[0][None], outs[1][None], outs[2], outs[3])


def solution(mesh):
    in_specs = (
        P("dp", ("sample", "head"), None),
        P("dp", ("sample", "head"), None),
        P("dp", "sample", None, None),
        P("dp", "sample", None, None),
        P("dp", "sample", None, "head"),
        P("dp", "sample", None, "head"),
        P("dp", "sample", None, "head"),
        P("dp", "sample"),
        P(None, "head"),
        P(None, "head"),
    )
    out_specs = (
        P("dp", ("sample", "head"), None),
        P("dp", ("sample", "head"), None),
        P(("dp", "sample"), "head"),
        P(("dp", "sample"), "head"),
    )
    return jax.shard_map(local, mesh=mesh, in_specs=in_specs, out_specs=out_specs, check_vma=False)
```

```python
import math

import jax
import jax.numpy as jnp
from jax import lax
from jax.experimental import pallas as pl
from jax.experimental.pallas import tpu as pltpu
from jax.sharding import PartitionSpec as P

DH = 128
DR = 64
DC = 512
PLEN = 512
CLEN = 256
KEYS = PLEN + CLEN
WIDE = 640
ACOLS = 384
BCOLS = WIDE - ACOLS
PACK = 384
PAIRS = 8
STEPS = PAIRS // 2
NT = (((1,), (1,)), ((), ()))
SCALE = 1.0 / (DH + DR) ** 0.5
F32 = jnp.float32
BF16 = jnp.bfloat16
MESH = pl.DeviceIdType.MESH
OVER_XY = ((0, 0), (2, 0), (0, 1), (0, 3), (2, 1), (2, 3), (0, 2), (2, 2))
OVER_Z = (0, 1, 7, 2, 6, 3, 5, 4)
ALL_XY = tuple((dx, dy) for dx in range(4) for dy in range(4) if dx or dy)


def kernel(
    len_hbm, plat_hbm, prope_hbm, clat_hbm, crope_hbm, q_hbm, qr_hbm, g_hbm, wk_hbm, wv_hbm,
    glat_ref, gw_ref,
    plat, prope, clat, crope, q_ref, qr_ref, g_ref, wk_ref, wv_ref, len_ref,
    gz, gl, gr, lat, lat_t, rsel, kv, dkv_a, dkv_b, lacc, racc,
    wpart, crecv, csum, krecv1, ksum, krecv2, vrecv1, vsum, vrecv2, apart, a1recv, a2src, a2own, a2recv, bpart, b1recv, b2src, b2recv,
    load, gz_send, gz_recv, gl_send, gl_recv, gr_send, gr_recv, c_send, c_recv,
    k1_send, k1_recv, k2_send, k2_recv, v1_send, v1_recv, v2_send, v2_recv,
    a1_send, a1_recv, a2_send, a2_recv, b1_send, b1_recv, b2_send, b2_recv,
):
    step = pl.program_id(0)
    dp, sample, z = lax.axis_index("dp"), lax.axis_index("sample"), lax.axis_index("head")
    x_lo, core = lax.div(dp, 2), lax.rem(dp, 2)
    y, x_hi = lax.div(sample, 2), lax.rem(sample, 2)
    x = x_hi * 2 + x_lo

    def at_xy(dx, dy):
        to = lax.rem(x + dx, 4)
        return {"dp": lax.rem(to, 2) * 2 + core, "sample": lax.rem(y + dy, 4) * 2 + lax.div(to, 2)}

    def at_z(d):
        return {"head": lax.rem(z + d, 8)}

    other_core = {"dp": x_lo * 2 + 1 - core}

    def remote(src, dst, send, recv, device):
        return pltpu.make_async_remote_copy(
            src_ref=src, dst_ref=dst, send_sem=send, recv_sem=recv, device_id=device, device_id_type=MESH
        )

    def arrived(ref, sem):
        pltpu.make_async_copy(ref, ref, sem).wait()

    def swap_core(i):
        return remote(wpart.at[i, :, 1 - core], crecv.at[i], c_send.at[i], c_recv.at[i], other_core)

    def project(first, count):
        rows = lat[first : first + count, :, :DC].reshape(count * 64, DC)

        for i in range(PAIRS):
            cols = slice(i * 256, (i + 1) * 256)
            for half, w in enumerate((wk_ref, wv_ref)):
                kv[i, half, first * 64 : (first + count) * 64] = jnp.dot(
                    rows, w[:, cols], preferred_element_type=F32
                ).astype(BF16)
        tokens = slice(first * 64, (first + count) * 64)
        lat_t[:, tokens] = rows.T
        rope = lat[first : first + count, :, DC:].reshape(count * 64, DH)
        rsel[0, tokens] = rope
        rsel[1, tokens] = jnp.concatenate([jnp.zeros((count * 64, DR), BF16), rope[:, :DR]], 1)

    @pl.when(step == 0)
    def _():
        pairs = (
            (plat_hbm, plat), (prope_hbm, prope), (clat_hbm, clat), (crope_hbm, crope), (wk_hbm, wk_ref),
            (wv_hbm, wv_ref), (q_hbm, q_ref), (qr_hbm, qr_ref), (g_hbm, g_ref), (len_hbm, len_ref),
        )
        loads = [pltpu.make_async_copy(src, dst, load.at[n]) for n, (src, dst) in enumerate(pairs)]
        for copy in loads:
            copy.start()
        barrier = pltpu.get_barrier_semaphore()
        peers = [other_core] + [at_xy(dx, dy) for dx, dy in ALL_XY] + [at_z(d) for d in range(1, 8)]
        for peer in peers:
            pl.semaphore_signal(barrier, inc=1, device_id=peer, device_id_type=MESH)
        loads[0].wait()
        loads[1].wait()
        wide = plat[...].astype(F32)
        rope = jnp.concatenate([prope[...].astype(F32), jnp.zeros((8, DH - DR), F32)], 1)
        gz[0] = jnp.concatenate(
            [jnp.concatenate([wide[:, :256], wide[:, 256:]], 0), jnp.concatenate([rope, jnp.zeros((8, DH), F32)], 0)], 1
        ).astype(BF16)
        pl.semaphore_wait(barrier, len(peers))
        for k in range(1, 8):
            remote(gz.at[0], gz.at[k], gz_send, gz_recv.at[k // 5], at_z(8 - OVER_Z[k])).start()

        def forward(first, count):
            for b in range(1, 8):
                dx, dy = OVER_XY[b]
                blocks = pl.ds(first, count)
                remote(
                    gz.at[blocks, :, pl.ds(0, 256)], gl.at[b, blocks], gl_send, gl_recv.at[b // 4], at_xy(4 - dx, 4 - dy)
                ).start()

        def unpack(first, count):
            block = gl[first : first + count].astype(F32)
            block = jnp.concatenate([block[:, :, :8], block[:, :, 8:]], 3)
            lat[first : first + count, :, :DC] = block.reshape(count, 64, DC).astype(BF16)
            for b in range(first, first + count):
                rope = gr[b].astype(F32)
                rope = jnp.concatenate([rope[:, :DR], rope[:, DR:]], 0)
                lat[b, :, DC:] = jnp.concatenate([rope, jnp.zeros((64, DH - DR), F32)], 1).astype(BF16)

        forward(0, 1)
        loads[2].wait()
        loads[3].wait()
        lat[8:12, :, :DC] = clat[...].reshape(4, 64, DC)
        rope = jnp.concatenate([crope[...].astype(F32).T, jnp.zeros((CLEN, WIDE - DC - DR), F32)], 1)
        lat[8:12, :, DC:] = rope.astype(BF16).reshape(4, 64, WIDE - DC)
        loads[4].wait()
        loads[5].wait()
        project(8, 4)
        arrived(gz.at[pl.ds(1, 4)], gz_recv.at[0])
        forward(1, 4)
        dkv_b[...] = jnp.zeros_like(dkv_b)
        lacc[...] = jnp.zeros_like(lacc)
        racc[...] = jnp.zeros_like(racc)
        arrived(gz.at[pl.ds(5, 3)], gz_recv.at[1])
        forward(5, 3)
        rope = gz[:, :, 256:].astype(F32)[:, :8, :DR].reshape(64, DR)
        gr[0] = jnp.concatenate([rope[:32], rope[32:]], 1).astype(BF16)
        for b in range(1, 8):
            dx, dy = OVER_XY[b]
            remote(gr.at[0], gr.at[b], gr_send, gr_recv.at[b // 4], at_xy(4 - dx, 4 - dy)).start()
        gl[0] = gz[:, :, :256]
        for copy in loads[6:]:
            copy.wait()
        live = lax.broadcasted_iota(jnp.int32, g_ref.shape, 0) < len_ref[...]
        g_ref[...] = jnp.where(live, g_ref[...], jnp.zeros((), BF16))
        arrived(gl.at[pl.ds(1, 3)], gl_recv.at[0])
        arrived(gr.at[pl.ds(1, 3)], gr_recv.at[0])
        unpack(0, 4)
        project(0, 4)
        arrived(gl.at[pl.ds(4, 4)], gl_recv.at[1])
        arrived(gr.at[pl.ds(4, 4)], gr_recv.at[1])
        unpack(4, 4)
        project(4, 4)
        arrived(gz.at[pl.ds(1, 7)], gz_send)
        arrived(gl.at[pl.ds(1, 7)], gl_send)
        arrived(gr.at[pl.ds(1, 7)], gr_send)

    def weights_of(i, dkv):
        part = jnp.dot(lat_t[...], dkv[...], preferred_element_type=F32).astype(BF16)
        wpart[i] = part.reshape(2, 2, 4, 2, 16, 512)

    def latents_of(i, dkv):
        cols = pl.ds(pl.multiple_of(i * 256, 256), 256)
        both = jnp.concatenate([wk_ref[:, cols], wv_ref[:, cols]], 1)
        lacc[...] += lax.dot_general(dkv[:PLEN], both, NT, preferred_element_type=F32)

    def add_core(i):
        swap_core(i).wait()
        for lo in range(2):
            total = wpart[i, lo, core].astype(F32) + crecv[i, lo].astype(F32)
            csum[i, 0, lo] = total[..., :256].astype(BF16)
            csum[i, 1, lo] = total[..., 256:].astype(BF16)
        for d in (1, 2, 3):
            to = lax.rem(x + d, 4)
            remote(csum.at[i, 0, lax.rem(to, 2), :, lax.div(to, 2)], krecv1.at[i, d - 1], k1_send.at[i], k1_recv.at[i], at_xy(d, 0)).start()
            remote(csum.at[i, 1, :, lax.rem(y + d, 4)], vrecv1.at[i, d - 1], v1_send.at[i], v1_recv.at[i], at_xy(0, d)).start()

    def add_first(i):
        arrived(krecv1.at[i], k1_recv.at[i])
        arrived(vrecv1.at[i], v1_recv.at[i])
        k = csum[i, 0, x_lo, :, x_hi].astype(F32)
        v = csum[i, 1, :, y].astype(F32)
        for d in range(3):
            k = k + krecv1[i, d].astype(F32)
            v = v + vrecv1[i, d].astype(F32)
        ksum[i] = k.astype(BF16)
        vsum[i] = v.astype(BF16)
        for d in (1, 2, 3):
            to = lax.rem(x + d, 4)
            remote(ksum.at[i, lax.rem(y + d, 4)], krecv2.at[i, d - 1], k2_send.at[i], k2_recv.at[i], at_xy(0, d)).start()
            remote(vsum.at[i, lax.rem(to, 2), lax.div(to, 2)], vrecv2.at[i, d - 1], v2_send.at[i], v2_recv.at[i], at_xy(d, 0)).start()

    def add_owned(i):
        arrived(krecv2.at[i], k2_recv.at[i])
        arrived(vrecv2.at[i], v2_recv.at[i])
        k = ksum[i, y].astype(F32)
        v = vsum[i, x_lo, x_hi].astype(F32)
        for d in range(3):
            k = k + krecv2[i, d].astype(F32)
            v = v + vrecv2[i, d].astype(F32)
        cols = pl.ds(pl.multiple_of(i * 256, 256), 256)
        gw_ref[0, :, cols] = k
        gw_ref[1, :, cols] = v
        arrived(krecv1.at[i], k1_send.at[i])
        arrived(vrecv1.at[i], v1_send.at[i])
        arrived(krecv2.at[i], k2_send.at[i])
        arrived(vrecv2.at[i], v2_send.at[i])

    see = lax.broadcasted_iota(jnp.int32, (CLEN, CLEN), 0) <= lax.broadcasted_iota(jnp.int32, (CLEN, CLEN), 1)

    last = PAIRS - 1

    def scores(i, h):
        start = pl.multiple_of(i * 256, 256) + h * DH
        mine = pl.ds(pl.multiple_of(start, DH), DH)
        cols = slice(h * DH, (h + 1) * DH)
        kx = jnp.concatenate([kv[i, 0, :, cols], rsel[h]], 1)
        qx = jnp.concatenate([q_ref[:, mine], qr_ref[:, pl.ds(pl.multiple_of(i * DH, DH), DH)]], 1)
        g = g_ref[:, mine]
        s = lax.dot_general(kx, qx, NT, preferred_element_type=F32)
        dprob = lax.dot_general(kv[i, 1, :, cols], g, NT, preferred_element_type=F32)
        return qx, g, s, dprob

    def gradients(h, new, qx, g, s, dprob):
        s = jnp.concatenate([s[:PLEN], jnp.where(see, s[PLEN:], -1e30)], 0)
        m = jnp.max(s, axis=0, keepdims=True)
        p = jnp.exp2((s - m) * (SCALE * math.log2(math.e)))
        p = p * (1.0 / jnp.sum(p, axis=0, keepdims=True))
        pb = p.astype(BF16)
        new[:, 256 + h * DH : 256 + (h + 1) * DH] = jnp.dot(pb, g, preferred_element_type=F32).astype(BF16)
        delta = jnp.sum(pb.astype(F32) * dprob, axis=0, keepdims=True)
        ds = (p * (dprob - delta)).astype(BF16)
        dk = jnp.dot(ds, qx, preferred_element_type=F32)
        new[:, h * DH : (h + 1) * DH] = (dk[:, :DH] * SCALE).astype(BF16)
        racc[h] += dk[:PLEN, DH:]

    def attend(i, new, before, old):
        one = scores(i, 0)
        weights_of(before, old)
        two = scores(i, 1)
        latents_of(before, old)
        gradients(0, new, *one)
        gradients(1, new, *two)

    def grads_of_head(h):
        return jnp.concatenate([dkv_b[:, h * DH : (h + 1) * DH], dkv_b[:, 256 + h * DH : 256 + (h + 1) * DH]], 1)

    def weights_of_head(h):
        part = jnp.dot(lat_t[...], grads_of_head(h), preferred_element_type=F32).astype(BF16)
        for n in range(2):
            cols = slice(n * 256 + h * DH, n * 256 + (h + 1) * DH)
            wpart[last, :, :, :, :, :, cols] = part[:, n * DH : (n + 1) * DH].reshape(2, 2, 4, 2, 16, DH)

    def latents_of_head(h):
        mine = slice(last * 256 + h * DH, last * 256 + (h + 1) * DH)
        both = jnp.concatenate([wk_ref[:, mine], wv_ref[:, mine]], 1)
        lacc[...] += lax.dot_general(grads_of_head(h)[:PLEN], both, NT, preferred_element_type=F32)

    first, second = 2 * step, 2 * step + 1
    attend(first, dkv_a, jnp.maximum(first - 1, 0), dkv_b)

    @pl.when(step >= 1)
    def _():
        swap_core(first - 1).start()
        add_core(first - 2)

    @pl.when(step >= 2)
    def _():
        add_first(first - 4)

    @pl.when(step >= 3)
    def _():
        add_owned(first - 6)

    @pl.when(step < STEPS - 1)
    def _():
        attend(second, dkv_b, first, dkv_a)
        swap_core(first).start()

    @pl.when((step >= 1) & (step < STEPS - 1))
    def _():
        add_core(first - 1)

    @pl.when((step >= 2) & (step < STEPS - 1))
    def _():
        add_first(first - 3)

    @pl.when(step == STEPS - 1)
    def _():
        head = scores(last, 0)
        weights_of(last - 1, dkv_a)
        latents_of(last - 1, dkv_a)
        gradients(0, dkv_b, *head)
        swap_core(last - 1).start()
        add_core(last - 2)
        add_first(last - 4)

    @pl.when(step == STEPS - 1)
    def _():
        head = scores(last, 1)
        weights_of_head(0)
        latents_of_head(0)
        gradients(1, dkv_b, *head)

    @pl.when(step == STEPS - 1)
    def _():
        latents_of_head(1)
        apart[...] = lacc[:, :ACOLS].astype(BF16).reshape(8, 64, ACOLS)
        for b in range(1, 8):
            remote(apart.at[b], a1recv.at[b - 1], a1_send, a1_recv, at_xy(*OVER_XY[b])).start()
        weights_of_head(1)
        swap_core(last).start()
        add_core(last - 1)
        rope = (racc[0, :, :DR] + racc[1, :, DR:]) * SCALE
        rest = lacc[:, ACOLS:]
        for k in range(8):
            mine = [slice(b * 64 + k * 8, b * 64 + k * 8 + 8) for b in range(8)]
            left = jnp.concatenate([rope[rows] for rows in mine[:4]], 0)
            right = jnp.concatenate([rope[rows] for rows in mine[4:]], 0)
            both = jnp.concatenate([left, right], 1)
            bpart[k] = jnp.concatenate([rest[rows] for rows in mine] + [both], 0).astype(BF16)
        for k in range(1, 8):
            remote(bpart.at[k], b1recv.at[k - 1], b1_send, b1_recv, at_z(OVER_Z[k])).start()
        add_core(last)
        add_first(last - 3)
        add_owned(last - 6)
        add_owned(last - 5)
        add_first(last - 2)
        add_first(last - 1)
        arrived(a1recv, a1_recv)
        total = apart[0].astype(F32)
        for b in range(7):
            total = total + a1recv[b].astype(F32)
        total = total.reshape(8, 8, ACOLS)
        a2own[...] = total[0]
        right = jnp.concatenate([total[:, :, 256:], jnp.zeros((8, 8, 512 - ACOLS), F32)], 2)
        a2src[...] = jnp.concatenate([total[:, :, :256], right], 1).astype(BF16)
        for k in range(1, 8):
            remote(a2src.at[k], a2recv.at[k - 1], a2_send, a2_recv, at_z(OVER_Z[k])).start()
        add_first(last)
        arrived(b1recv, b1_recv)
        total = bpart[0].astype(F32)
        for k in range(7):
            total = total + b1recv[k].astype(F32)
        rope = jnp.concatenate([total[64:, :DR], total[64:, DR:]], 0)
        rope = jnp.concatenate([rope, jnp.zeros((64, DH - DR), F32)], 1)
        b2src[...] = jnp.concatenate([total[:64], rope], 1).reshape(8, 8, BCOLS)
        for b in range(1, 8):
            remote(b2src.at[b], b2recv.at[b - 1], b2_send, b2_recv, at_xy(*OVER_XY[b])).start()
        for i in range(last - 4, last + 1):
            add_owned(i)
        arrived(a2recv, a2_recv)
        total = a2recv[0].astype(F32)
        for k in range(1, 7):
            total = total + a2recv[k].astype(F32)
        glat_ref[:, :256] = a2own[:, :256] + total[:8]
        glat_ref[:, 256:ACOLS] = a2own[:, 256:] + total[8:, : ACOLS - 256]
        arrived(b2recv, b2_recv)
        total = b2src[0]
        for b in range(7):
            total = total + b2recv[b]
        glat_ref[:, ACOLS:] = total
        arrived(a1recv, a1_send)
        arrived(b1recv, b1_send)
        arrived(a2recv, a2_send)
        arrived(b2recv, b2_send)


def finish(lat_ref, w_ref, glat_ref, grope_ref, gwk_ref, gwv_ref):
    glat_ref[...] = lat_ref[:, :DC]
    grope_ref[...] = lat_ref[:, DC : DC + DR]
    gwk_ref[...] = w_ref[0]
    gwv_ref[...] = w_ref[1]


def local(prompt_latent, prompt_rope, comp_latent, comp_rope, query_nope, query_rope, grad_out, lengths, w_uk, w_uv):
    def whole(*shape):
        return pl.BlockSpec(shape, lambda i: (0,) * len(shape))

    vmem, dma = pltpu.VMEM, pltpu.SemaphoreType.DMA
    lat, weights = pl.pallas_call(
        kernel,
        grid=(STEPS,),
        in_specs=[pl.BlockSpec(memory_space=pl.ANY)] * 10,
        out_specs=[whole(8, WIDE), whole(2, 16, 2048)],
        out_shape=[jax.ShapeDtypeStruct((8, WIDE), F32), jax.ShapeDtypeStruct((2, 16, 2048), F32)],
        scratch_shapes=[
            vmem((8, DC), BF16), vmem((8, DR), BF16), vmem((CLEN, DC), BF16), vmem((DR, CLEN), BF16),
            vmem((CLEN, 2048), BF16), vmem((CLEN, 1024), BF16), vmem((CLEN, 2048), BF16),
            vmem((DC, 2048), BF16), vmem((DC, 2048), BF16), vmem((1, 1), jnp.int32),
            vmem((8, 16, PACK), BF16), vmem((8, 8, 16, 256), BF16), vmem((8, 32, DH), BF16),
            vmem((12, 64, WIDE), BF16), vmem((DC, KEYS), BF16), vmem((2, KEYS, DH), BF16),
            vmem((PAIRS, 2, KEYS, 256), BF16), vmem((KEYS, 512), BF16), vmem((KEYS, 512), BF16),
            vmem((PLEN, DC), F32), vmem((2, PLEN, DH), F32),
            vmem((PAIRS, 2, 2, 4, 2, 16, 512), BF16),
            vmem((PAIRS, 2, 4, 2, 16, 512), BF16),
            vmem((PAIRS, 2, 2, 4, 2, 16, 256), BF16),
            vmem((PAIRS, 3, 4, 16, 256), BF16), vmem((PAIRS, 4, 16, 256), BF16), vmem((PAIRS, 3, 16, 256), BF16),
            vmem((PAIRS, 3, 2, 2, 16, 256), BF16), vmem((PAIRS, 2, 2, 16, 256), BF16), vmem((PAIRS, 3, 16, 256), BF16),
            vmem((8, 64, ACOLS), BF16), vmem((7, 64, ACOLS), BF16), vmem((8, 16, 256), BF16), vmem((8, ACOLS), F32), vmem((7, 16, 256), BF16),
            vmem((8, 96, DH), BF16), vmem((7, 96, DH), BF16), vmem((8, 8, BCOLS), F32), vmem((7, 8, BCOLS), F32),
            dma((10,)), dma, dma((2,)), dma, dma((2,)), dma, dma((2,)),
            *[dma((PAIRS,))] * 10, *[dma] * 8,
        ],
        compiler_params=pltpu.CompilerParams(
            vmem_limit_bytes=56 * 1024 * 1024, collective_id=0, has_side_effects=True
        ),
        cost_estimate=pl.CostEstimate(flops=13_000_000_000, bytes_accessed=8_000_000, transcendentals=3_200_000),
        name="mla_backward",
    )(
        lengths, prompt_latent[0], prompt_rope[0], comp_latent[0, 0], comp_rope[0, 0].T,
        query_nope[0, 0], query_rope[0, 0], grad_out[0, 0], w_uk, w_uv,
    )
    outs = pl.pallas_call(
        finish,
        out_shape=[
            jax.ShapeDtypeStruct((8, DC), F32), jax.ShapeDtypeStruct((8, DR), F32),
            jax.ShapeDtypeStruct((16, 2048), F32), jax.ShapeDtypeStruct((16, 2048), F32),
        ],
        name="outputs",
    )(lat, weights)
    return (outs[0][None], outs[1][None], outs[2], outs[3])


def solution(mesh):
    in_specs = (
        P("dp", ("sample", "head"), None),
        P("dp", ("sample", "head"), None),
        P("dp", "sample", None, None),
        P("dp", "sample", None, None),
        P("dp", "sample", None, "head"),
        P("dp", "sample", None, "head"),
        P("dp", "sample", None, "head"),
        P("dp", "sample"),
        P(None, "head"),
        P(None, "head"),
    )
    out_specs = (
        P("dp", ("sample", "head"), None),
        P("dp", ("sample", "head"), None),
        P(("dp", "sample"), "head"),
        P(("dp", "sample"), "head"),
    )
    return jax.shard_map(local, mesh=mesh, in_specs=in_specs, out_specs=out_specs, check_vma=False)
```

```python
import math

import jax
import jax.numpy as jnp
from jax import lax
from jax.experimental import pallas as pl
from jax.experimental.pallas import tpu as pltpu
from jax.sharding import PartitionSpec as P

DH = 128
DR = 64
DC = 512
PLEN = 512
CLEN = 256
KEYS = PLEN + CLEN
WIDE = 640
ACOLS = 384
BCOLS = WIDE - ACOLS
PACK = 384
PAIRS = 8
STEPS = PAIRS // 2
NT = (((1,), (1,)), ((), ()))
SCALE = 1.0 / (DH + DR) ** 0.5
F32 = jnp.float32
BF16 = jnp.bfloat16
MESH = pl.DeviceIdType.MESH
OVER_XY = ((0, 0), (2, 0), (0, 1), (0, 3), (2, 1), (2, 3), (0, 2), (2, 2))
OVER_Z = (0, 1, 7, 2, 6, 3, 5, 4)
ALL_XY = tuple((dx, dy) for dx in range(4) for dy in range(4) if dx or dy)


def kernel(
    len_hbm, plat_hbm, prope_hbm, clat_hbm, crope_hbm, q_hbm, qr_hbm, g_hbm, wk_hbm, wv_hbm,
    glat_ref, gw_ref,
    plat, prope, clat, crope, q_ref, qr_ref, g_ref, wk_ref, wv_ref, len_ref,
    gz, gl, gr, lat, lat_t, rsel, kv, dkv_a, dkv_b, lacc, racc,
    wpart, crecv, csum, krecv1, ksum, krecv2, vrecv1, vsum, vrecv2, apart, a1recv, a2src, a2own, a2recv, bpart, b1recv, b2src, b2recv,
    load, gz_send, gz_recv, gl_send, gl_recv, gr_send, gr_recv, c_send, c_recv,
    k1_send, k1_recv, k2_send, k2_recv, v1_send, v1_recv, v2_send, v2_recv,
    a1_send, a1_recv, a2_send, a2_recv, b1_send, b1_recv, b2_send, b2_recv,
):
    step = pl.program_id(0)
    dp, sample, z = lax.axis_index("dp"), lax.axis_index("sample"), lax.axis_index("head")
    x_lo, core = lax.div(dp, 2), lax.rem(dp, 2)
    y, x_hi = lax.div(sample, 2), lax.rem(sample, 2)
    x = x_hi * 2 + x_lo

    def at_xy(dx, dy):
        to = lax.rem(x + dx, 4)
        return {"dp": lax.rem(to, 2) * 2 + core, "sample": lax.rem(y + dy, 4) * 2 + lax.div(to, 2)}

    def at_z(d):
        return {"head": lax.rem(z + d, 8)}

    other_core = {"dp": x_lo * 2 + 1 - core}

    def remote(src, dst, send, recv, device):
        return pltpu.make_async_remote_copy(
            src_ref=src, dst_ref=dst, send_sem=send, recv_sem=recv, device_id=device, device_id_type=MESH
        )

    def arrived(ref, sem):
        pltpu.make_async_copy(ref, ref, sem).wait()

    def swap_core(i):
        return remote(wpart.at[i, :, 1 - core], crecv.at[i], c_send.at[i], c_recv.at[i], other_core)

    def project(first, count, pairs=range(PAIRS)):
        rows = lat[first : first + count, :, :DC].reshape(count * 64, DC)
        for i in pairs:
            cols = slice(i * 256, (i + 1) * 256)
            for half, w in enumerate((wk_ref, wv_ref)):
                kv[i, half, first * 64 : (first + count) * 64] = jnp.dot(
                    rows, w[:, cols], preferred_element_type=F32
                ).astype(BF16)

    def place(first, count):
        tokens = slice(first * 64, (first + count) * 64)
        lat_t[:, tokens] = lat[first : first + count, :, :DC].reshape(count * 64, DC).T
        rope = lat[first : first + count, :, DC:].reshape(count * 64, DH)
        rsel[0, tokens] = rope
        rsel[1, tokens] = jnp.concatenate([jnp.zeros((count * 64, DR), BF16), rope[:, :DR]], 1)

    @pl.when(step == 0)
    def _():
        pairs = (
            (plat_hbm, plat), (prope_hbm, prope), (clat_hbm, clat), (crope_hbm, crope), (wk_hbm, wk_ref),
            (wv_hbm, wv_ref), (q_hbm, q_ref), (qr_hbm, qr_ref), (g_hbm, g_ref), (len_hbm, len_ref),
        )
        loads = [pltpu.make_async_copy(src, dst, load.at[n]) for n, (src, dst) in enumerate(pairs)]
        for copy in loads:
            copy.start()
        barrier = pltpu.get_barrier_semaphore()
        peers = [other_core] + [at_xy(dx, dy) for dx, dy in ALL_XY] + [at_z(d) for d in range(1, 8)]
        for peer in peers:
            pl.semaphore_signal(barrier, inc=1, device_id=peer, device_id_type=MESH)
        loads[0].wait()
        loads[1].wait()
        wide = plat[...].astype(F32)
        rope = jnp.concatenate([prope[...].astype(F32), jnp.zeros((8, DH - DR), F32)], 1)
        gz[0] = jnp.concatenate(
            [jnp.concatenate([wide[:, :256], wide[:, 256:]], 0), jnp.concatenate([rope, jnp.zeros((8, DH), F32)], 0)], 1
        ).astype(BF16)
        pl.semaphore_wait(barrier, len(peers))
        for k in range(1, 8):
            remote(gz.at[0], gz.at[k], gz_send, gz_recv.at[k // 5], at_z(8 - OVER_Z[k])).start()

        def forward(first, count):
            for b in range(1, 8):
                dx, dy = OVER_XY[b]
                blocks = pl.ds(first, count)
                remote(
                    gz.at[blocks, :, pl.ds(0, 256)], gl.at[b, blocks], gl_send, gl_recv.at[b // 4], at_xy(4 - dx, 4 - dy)
                ).start()

        def unpack(first, count):
            block = gl[first : first + count].astype(F32)
            block = jnp.concatenate([block[:, :, :8], block[:, :, 8:]], 3)
            lat[first : first + count, :, :DC] = block.reshape(count, 64, DC).astype(BF16)
            for b in range(first, first + count):
                rope = gr[b].astype(F32)
                rope = jnp.concatenate([rope[:, :DR], rope[:, DR:]], 0)
                lat[b, :, DC:] = jnp.concatenate([rope, jnp.zeros((64, DH - DR), F32)], 1).astype(BF16)

        forward(0, 1)
        loads[2].wait()
        loads[3].wait()
        lat[8:12, :, :DC] = clat[...].reshape(4, 64, DC)
        rope = jnp.concatenate([crope[...].astype(F32).T, jnp.zeros((CLEN, WIDE - DC - DR), F32)], 1)
        lat[8:12, :, DC:] = rope.astype(BF16).reshape(4, 64, WIDE - DC)
        loads[4].wait()
        loads[5].wait()
        project(8, 4)
        place(8, 4)
        arrived(gz.at[pl.ds(1, 4)], gz_recv.at[0])
        forward(1, 4)
        lacc[...] = jnp.zeros_like(lacc)
        racc[...] = jnp.zeros_like(racc)
        arrived(gz.at[pl.ds(5, 3)], gz_recv.at[1])
        forward(5, 3)
        rope = gz[:, :, 256:].astype(F32)[:, :8, :DR].reshape(64, DR)
        gr[0] = jnp.concatenate([rope[:32], rope[32:]], 1).astype(BF16)
        for b in range(1, 8):
            dx, dy = OVER_XY[b]
            remote(gr.at[0], gr.at[b], gr_send, gr_recv.at[b // 4], at_xy(4 - dx, 4 - dy)).start()
        gl[0] = gz[:, :, :256]
        for copy in loads[6:]:
            copy.wait()
        live = lax.broadcasted_iota(jnp.int32, g_ref.shape, 0) < len_ref[...]
        g_ref[...] = jnp.where(live, g_ref[...], jnp.zeros((), BF16))
        arrived(gl.at[pl.ds(1, 3)], gl_recv.at[0])
        arrived(gr.at[pl.ds(1, 3)], gr_recv.at[0])
        unpack(0, 4)
        project(0, 4)
        place(0, 4)
        arrived(gl.at[pl.ds(4, 4)], gl_recv.at[1])
        arrived(gr.at[pl.ds(4, 4)], gr_recv.at[1])
        unpack(4, 4)
        project(4, 4, (0,))
        place(4, 4)
        arrived(gz.at[pl.ds(1, 7)], gz_send)
        arrived(gl.at[pl.ds(1, 7)], gl_send)
        arrived(gr.at[pl.ds(1, 7)], gr_send)

    def weights_of(i, dkv):
        part = jnp.dot(lat_t[...], dkv[...], preferred_element_type=F32).astype(BF16)
        wpart[i] = part.reshape(2, 2, 4, 2, 16, 512)

    def latents_of(i, dkv):
        cols = pl.ds(pl.multiple_of(i * 256, 256), 256)
        both = jnp.concatenate([wk_ref[:, cols], wv_ref[:, cols]], 1)
        lacc[...] += lax.dot_general(dkv[:PLEN], both, NT, preferred_element_type=F32)

    def add_core(i):
        swap_core(i).wait()
        for lo in range(2):
            total = wpart[i, lo, core].astype(F32) + crecv[i, lo].astype(F32)
            csum[i, 0, lo] = total[..., :256].astype(BF16)
            csum[i, 1, lo] = total[..., 256:].astype(BF16)
        for d in (1, 2, 3):
            to = lax.rem(x + d, 4)
            remote(csum.at[i, 0, lax.rem(to, 2), :, lax.div(to, 2)], krecv1.at[i, d - 1], k1_send.at[i], k1_recv.at[i], at_xy(d, 0)).start()
            remote(csum.at[i, 1, :, lax.rem(y + d, 4)], vrecv1.at[i, d - 1], v1_send.at[i], v1_recv.at[i], at_xy(0, d)).start()

    def add_first(i):
        arrived(krecv1.at[i], k1_recv.at[i])
        arrived(vrecv1.at[i], v1_recv.at[i])
        k = csum[i, 0, x_lo, :, x_hi].astype(F32)
        v = csum[i, 1, :, y].astype(F32)
        for d in range(3):
            k = k + krecv1[i, d].astype(F32)
            v = v + vrecv1[i, d].astype(F32)
        ksum[i] = k.astype(BF16)
        vsum[i] = v.astype(BF16)
        for d in (1, 2, 3):
            to = lax.rem(x + d, 4)
            remote(ksum.at[i, lax.rem(y + d, 4)], krecv2.at[i, d - 1], k2_send.at[i], k2_recv.at[i], at_xy(0, d)).start()
            remote(vsum.at[i, lax.rem(to, 2), lax.div(to, 2)], vrecv2.at[i, d - 1], v2_send.at[i], v2_recv.at[i], at_xy(d, 0)).start()

    def add_owned(i):
        arrived(krecv2.at[i], k2_recv.at[i])
        arrived(vrecv2.at[i], v2_recv.at[i])
        k = ksum[i, y].astype(F32)
        v = vsum[i, x_lo, x_hi].astype(F32)
        for d in range(3):
            k = k + krecv2[i, d].astype(F32)
            v = v + vrecv2[i, d].astype(F32)
        cols = pl.ds(pl.multiple_of(i * 256, 256), 256)
        gw_ref[0, :, cols] = k
        gw_ref[1, :, cols] = v
        arrived(krecv1.at[i], k1_send.at[i])
        arrived(vrecv1.at[i], v1_send.at[i])
        arrived(krecv2.at[i], k2_send.at[i])
        arrived(vrecv2.at[i], v2_send.at[i])

    see = lax.broadcasted_iota(jnp.int32, (CLEN, CLEN), 0) <= lax.broadcasted_iota(jnp.int32, (CLEN, CLEN), 1)

    last = PAIRS - 1

    def scores(i, h):
        mine = pl.ds(pl.multiple_of(i * 256 + h * DH, DH), DH)
        cols = slice(h * DH, (h + 1) * DH)
        kx = jnp.concatenate([kv[i, 0, :, cols], rsel[h]], 1)
        qx = jnp.concatenate([q_ref[:, mine], qr_ref[:, pl.ds(pl.multiple_of(i * DH, DH), DH)]], 1)
        g = g_ref[:, mine]
        s = lax.dot_general(kx, qx, NT, preferred_element_type=F32)
        dprob = lax.dot_general(kv[i, 1, :, cols], g, NT, preferred_element_type=F32)
        return qx, g, s, dprob

    def gradients(h, new, qx, g, s, dprob):
        s = jnp.concatenate([s[:PLEN], jnp.where(see, s[PLEN:], -1e30)], 0)
        m = jnp.max(s, axis=0, keepdims=True)
        p = jnp.exp2((s - m) * (SCALE * math.log2(math.e)))
        p = p * (1.0 / jnp.sum(p, axis=0, keepdims=True))
        pb = p.astype(BF16)
        new[:, 256 + h * DH : 256 + (h + 1) * DH] = jnp.dot(pb, g, preferred_element_type=F32).astype(BF16)
        delta = jnp.sum(pb.astype(F32) * dprob, axis=0, keepdims=True)
        ds = (p * (dprob - delta)).astype(BF16)
        dk = jnp.dot(ds, qx, preferred_element_type=F32)
        new[:, h * DH : (h + 1) * DH] = (dk[:, :DH] * SCALE).astype(BF16)
        racc[h] += dk[:PLEN, DH:]

    def attend(i, new, before, old):
        one = scores(i, 0)
        weights_of(before, old)
        two = scores(i, 1)
        latents_of(before, old)
        gradients(0, new, *one)
        gradients(1, new, *two)

    def grads_of_head(h):
        return jnp.concatenate([dkv_b[:, h * DH : (h + 1) * DH], dkv_b[:, 256 + h * DH : 256 + (h + 1) * DH]], 1)

    def weights_of_head(h):
        part = jnp.dot(lat_t[...], grads_of_head(h), preferred_element_type=F32).astype(BF16)
        for n in range(2):
            cols = slice(n * 256 + h * DH, n * 256 + (h + 1) * DH)
            wpart[last, :, :, :, :, :, cols] = part[:, n * DH : (n + 1) * DH].reshape(2, 2, 4, 2, 16, DH)

    def latents_of_head(h):
        mine = slice(last * 256 + h * DH, last * 256 + (h + 1) * DH)
        both = jnp.concatenate([wk_ref[:, mine], wv_ref[:, mine]], 1)
        lacc[...] += lax.dot_general(grads_of_head(h)[:PLEN], both, NT, preferred_element_type=F32)

    first, second = 2 * step, 2 * step + 1

    @pl.when(step == 0)
    def _():
        one = scores(0, 0)
        two = scores(0, 1)
        project(4, 4, range(1, PAIRS))
        gradients(0, dkv_a, *one)
        gradients(1, dkv_a, *two)

    @pl.when(step >= 1)
    def _():
        attend(first, dkv_a, first - 1, dkv_b)
        swap_core(first - 1).start()
        add_core(first - 2)

    @pl.when(step >= 2)
    def _():
        add_first(first - 4)

    @pl.when(step >= 3)
    def _():
        add_owned(first - 6)

    @pl.when(step < STEPS - 1)
    def _():
        attend(second, dkv_b, first, dkv_a)
        swap_core(first).start()

    @pl.when((step >= 1) & (step < STEPS - 1))
    def _():
        add_core(first - 1)

    @pl.when((step >= 2) & (step < STEPS - 1))
    def _():
        add_first(first - 3)

    @pl.when(step == STEPS - 1)
    def _():
        head = scores(last, 0)
        weights_of(last - 1, dkv_a)
        latents_of(last - 1, dkv_a)
        gradients(0, dkv_b, *head)
        swap_core(last - 1).start()
        add_core(last - 2)
        add_first(last - 4)

    @pl.when(step == STEPS - 1)
    def _():
        head = scores(last, 1)
        weights_of_head(0)
        latents_of_head(0)
        gradients(1, dkv_b, *head)

    @pl.when(step == STEPS - 1)
    def _():
        latents_of_head(1)
        apart[...] = lacc[:, :ACOLS].astype(BF16).reshape(8, 64, ACOLS)
        for b in range(1, 8):
            remote(apart.at[b], a1recv.at[b - 1], a1_send, a1_recv, at_xy(*OVER_XY[b])).start()
        weights_of_head(1)
        swap_core(last).start()
        add_core(last - 1)
        rope = (racc[0, :, :DR] + racc[1, :, DR:]) * SCALE
        rest = lacc[:, ACOLS:]
        for k in range(8):
            mine = [slice(b * 64 + k * 8, b * 64 + k * 8 + 8) for b in range(8)]
            left = jnp.concatenate([rope[rows] for rows in mine[:4]], 0)
            right = jnp.concatenate([rope[rows] for rows in mine[4:]], 0)
            both = jnp.concatenate([left, right], 1)
            bpart[k] = jnp.concatenate([rest[rows] for rows in mine] + [both], 0).astype(BF16)
        for k in range(1, 8):
            remote(bpart.at[k], b1recv.at[k - 1], b1_send, b1_recv, at_z(OVER_Z[k])).start()
        add_core(last)
        add_first(last - 3)
        add_owned(last - 6)
        add_owned(last - 5)
        add_first(last - 2)
        arrived(a1recv, a1_recv)
        total = apart[0].astype(F32)
        for b in range(7):
            total = total + a1recv[b].astype(F32)
        total = total.reshape(8, 8, ACOLS)
        a2own[...] = total[0]
        right = jnp.concatenate([total[:, :, 256:], jnp.zeros((8, 8, 512 - ACOLS), F32)], 2)
        a2src[...] = jnp.concatenate([total[:, :, :256], right], 1).astype(BF16)
        for k in range(1, 8):
            remote(a2src.at[k], a2recv.at[k - 1], a2_send, a2_recv, at_z(OVER_Z[k])).start()
        add_first(last - 1)
        add_first(last)
        arrived(b1recv, b1_recv)
        total = bpart[0].astype(F32)
        for k in range(7):
            total = total + b1recv[k].astype(F32)
        rope = jnp.concatenate([total[64:, :DR], total[64:, DR:]], 0)
        rope = jnp.concatenate([rope, jnp.zeros((64, DH - DR), F32)], 1)
        b2src[...] = jnp.concatenate([total[:64], rope], 1).reshape(8, 8, BCOLS)
        for b in range(1, 8):
            remote(b2src.at[b], b2recv.at[b - 1], b2_send, b2_recv, at_xy(*OVER_XY[b])).start()
        lax.fori_loop(last - 4, last + 1, lambda i, c: (add_owned(i), c)[1], 0)
        arrived(a2recv, a2_recv)
        total = a2recv[0].astype(F32)
        for k in range(1, 7):
            total = total + a2recv[k].astype(F32)
        glat_ref[:, :256] = a2own[:, :256] + total[:8]
        glat_ref[:, 256:ACOLS] = a2own[:, 256:] + total[8:, : ACOLS - 256]
        arrived(b2recv, b2_recv)
        total = b2src[0]
        for b in range(7):
            total = total + b2recv[b]
        glat_ref[:, ACOLS:] = total
        arrived(a1recv, a1_send)
        arrived(b1recv, b1_send)
        arrived(a2recv, a2_send)
        arrived(b2recv, b2_send)


def finish(lat_ref, w_ref, glat_ref, grope_ref, gwk_ref, gwv_ref):
    glat_ref[...] = lat_ref[:, :DC]
    grope_ref[...] = lat_ref[:, DC : DC + DR]
    gwk_ref[...] = w_ref[0]
    gwv_ref[...] = w_ref[1]


def local(prompt_latent, prompt_rope, comp_latent, comp_rope, query_nope, query_rope, grad_out, lengths, w_uk, w_uv):
    def whole(*shape):
        return pl.BlockSpec(shape, lambda i: (0,) * len(shape))

    vmem, dma = pltpu.VMEM, pltpu.SemaphoreType.DMA
    lat, weights = pl.pallas_call(
        kernel,
        grid=(STEPS,),
        in_specs=[pl.BlockSpec(memory_space=pl.ANY)] * 10,
        out_specs=[whole(8, WIDE), whole(2, 16, 2048)],
        out_shape=[jax.ShapeDtypeStruct((8, WIDE), F32), jax.ShapeDtypeStruct((2, 16, 2048), F32)],
        scratch_shapes=[
            vmem((8, DC), BF16), vmem((8, DR), BF16), vmem((CLEN, DC), BF16), vmem((DR, CLEN), BF16),
            vmem((CLEN, 2048), BF16), vmem((CLEN, 1024), BF16), vmem((CLEN, 2048), BF16),
            vmem((DC, 2048), BF16), vmem((DC, 2048), BF16), vmem((1, 1), jnp.int32),
            vmem((8, 16, PACK), BF16), vmem((8, 8, 16, 256), BF16), vmem((8, 32, DH), BF16),
            vmem((12, 64, WIDE), BF16), vmem((DC, KEYS), BF16), vmem((2, KEYS, DH), BF16),
            vmem((PAIRS, 2, KEYS, 256), BF16), vmem((KEYS, 512), BF16), vmem((KEYS, 512), BF16),
            vmem((PLEN, DC), F32), vmem((2, PLEN, DH), F32),
            vmem((PAIRS, 2, 2, 4, 2, 16, 512), BF16),
            vmem((PAIRS, 2, 4, 2, 16, 512), BF16),
            vmem((PAIRS, 2, 2, 4, 2, 16, 256), BF16),
            vmem((PAIRS, 3, 4, 16, 256), BF16), vmem((PAIRS, 4, 16, 256), BF16), vmem((PAIRS, 3, 16, 256), BF16),
            vmem((PAIRS, 3, 2, 2, 16, 256), BF16), vmem((PAIRS, 2, 2, 16, 256), BF16), vmem((PAIRS, 3, 16, 256), BF16),
            vmem((8, 64, ACOLS), BF16), vmem((7, 64, ACOLS), BF16), vmem((8, 16, 256), BF16), vmem((8, ACOLS), F32), vmem((7, 16, 256), BF16),
            vmem((8, 96, DH), BF16), vmem((7, 96, DH), BF16), vmem((8, 8, BCOLS), F32), vmem((7, 8, BCOLS), F32),
            dma((10,)), dma, dma((2,)), dma, dma((2,)), dma, dma((2,)),
            *[dma((PAIRS,))] * 10, *[dma] * 8,
        ],
        compiler_params=pltpu.CompilerParams(
            vmem_limit_bytes=56 * 1024 * 1024, collective_id=0, has_side_effects=True
        ),
        cost_estimate=pl.CostEstimate(flops=13_000_000_000, bytes_accessed=8_000_000, transcendentals=3_200_000),
        name="mla_backward",
    )(
        lengths, prompt_latent[0], prompt_rope[0], comp_latent[0, 0], comp_rope[0, 0].T,
        query_nope[0, 0], query_rope[0, 0], grad_out[0, 0], w_uk, w_uv,
    )
    outs = pl.pallas_call(
        finish,
        out_shape=[
            jax.ShapeDtypeStruct((8, DC), F32), jax.ShapeDtypeStruct((8, DR), F32),
            jax.ShapeDtypeStruct((16, 2048), F32), jax.ShapeDtypeStruct((16, 2048), F32),
        ],
        name="outputs",
    )(lat, weights)
    return (outs[0][None], outs[1][None], outs[2], outs[3])


def solution(mesh):
    in_specs = (
        P("dp", ("sample", "head"), None),
        P("dp", ("sample", "head"), None),
        P("dp", "sample", None, None),
        P("dp", "sample", None, None),
        P("dp", "sample", None, "head"),
        P("dp", "sample", None, "head"),
        P("dp", "sample", None, "head"),
        P("dp", "sample"),
        P(None, "head"),
        P(None, "head"),
    )
    out_specs = (
        P("dp", ("sample", "head"), None),
        P("dp", ("sample", "head"), None),
        P(("dp", "sample"), "head"),
        P(("dp", "sample"), "head"),
    )
    return jax.shard_map(local, mesh=mesh, in_specs=in_specs, out_specs=out_specs, check_vma=False)
```

```python
import math

import jax
import jax.numpy as jnp
from jax import lax
from jax.experimental import pallas as pl
from jax.experimental.pallas import tpu as pltpu
from jax.sharding import PartitionSpec as P

DH = 128
DR = 64
DC = 512
PLEN = 512
CLEN = 256
KEYS = PLEN + CLEN
WIDE = 640
ACOLS = 384
BCOLS = WIDE - ACOLS
PACK = 384
PAIRS = 8
STEPS = PAIRS // 2
NT = (((1,), (1,)), ((), ()))
SCALE = 1.0 / (DH + DR) ** 0.5
F32 = jnp.float32
BF16 = jnp.bfloat16
MESH = pl.DeviceIdType.MESH
OVER_XY = ((0, 0), (2, 0), (0, 1), (0, 3), (2, 1), (2, 3), (0, 2), (2, 2))
OVER_Z = (0, 1, 7, 2, 6, 3, 5, 4)
ALL_XY = tuple((dx, dy) for dx in range(4) for dy in range(4) if dx or dy)


def kernel(
    len_hbm, plat_hbm, prope_hbm, clat_hbm, crope_hbm, q_hbm, qr_hbm, g_hbm, wk_hbm, wv_hbm,
    glat_ref, gw_ref,
    plat, prope, clat, crope, q_ref, qr_ref, g_ref, wk_ref, wv_ref, len_ref,
    gz, gl, gr, lat, lat_t, rsel, kv, dkv_a, dkv_b, lacc, racc,
    wpart, crecv, csum, krecv1, ksum, krecv2, vrecv1, vsum, vrecv2, apart, a1recv, a2src, a2own, a2recv, bpart, b1recv, b2src, b2recv,
    load, gz_send, gz_recv, gl_send, gl_recv, gr_send, gr_recv, c_send, c_recv,
    k1_send, k1_recv, k2_send, k2_recv, v1_send, v1_recv, v2_send, v2_recv,
    a1_send, a1_recv, a2_send, a2_recv, b1_send, b1_recv, b2_send, b2_recv,
):
    step = pl.program_id(0)
    dp, sample, z = lax.axis_index("dp"), lax.axis_index("sample"), lax.axis_index("head")
    x_lo, core = lax.div(dp, 2), lax.rem(dp, 2)
    y, x_hi = lax.div(sample, 2), lax.rem(sample, 2)
    x = x_hi * 2 + x_lo

    def at_xy(dx, dy):
        to = lax.rem(x + dx, 4)
        return {"dp": lax.rem(to, 2) * 2 + core, "sample": lax.rem(y + dy, 4) * 2 + lax.div(to, 2)}

    def at_z(d):
        return {"head": lax.rem(z + d, 8)}

    other_core = {"dp": x_lo * 2 + 1 - core}

    def remote(src, dst, send, recv, device):
        return pltpu.make_async_remote_copy(
            src_ref=src, dst_ref=dst, send_sem=send, recv_sem=recv, device_id=device, device_id_type=MESH
        )

    def arrived(ref, sem):
        pltpu.make_async_copy(ref, ref, sem).wait()

    def swap_core(i):
        return remote(wpart.at[i, :, 1 - core], crecv.at[i], c_send.at[i], c_recv.at[i], other_core)

    def project(first, count, pairs=range(PAIRS)):
        rows = lat[first : first + count, :, :DC].reshape(count * 64, DC)
        for i in pairs:
            cols = slice(i * 256, (i + 1) * 256)
            for half, w in enumerate((wk_ref, wv_ref)):
                kv[i, half, first * 64 : (first + count) * 64] = jnp.dot(
                    rows, w[:, cols], preferred_element_type=F32
                ).astype(BF16)

    def place(first, count):
        tokens = slice(first * 64, (first + count) * 64)
        lat_t[:, tokens] = lat[first : first + count, :, :DC].reshape(count * 64, DC).T
        rope = lat[first : first + count, :, DC:].reshape(count * 64, DH)
        rsel[0, tokens] = rope
        rsel[1, tokens] = jnp.concatenate([jnp.zeros((count * 64, DR), BF16), rope[:, :DR]], 1)

    @pl.when(step == 0)
    def _():
        pairs = (
            (plat_hbm, plat), (prope_hbm, prope), (clat_hbm, clat), (crope_hbm, crope), (wk_hbm, wk_ref),
            (wv_hbm, wv_ref), (q_hbm, q_ref), (qr_hbm, qr_ref), (g_hbm, g_ref), (len_hbm, len_ref),
        )
        loads = [pltpu.make_async_copy(src, dst, load.at[n]) for n, (src, dst) in enumerate(pairs)]
        for copy in loads:
            copy.start()
        barrier = pltpu.get_barrier_semaphore()
        peers = [other_core] + [at_xy(dx, dy) for dx, dy in ALL_XY] + [at_z(d) for d in range(1, 8)]
        for peer in peers:
            pl.semaphore_signal(barrier, inc=1, device_id=peer, device_id_type=MESH)
        loads[0].wait()
        loads[1].wait()
        wide = plat[...].astype(F32)
        rope = jnp.concatenate([prope[...].astype(F32), jnp.zeros((8, DH - DR), F32)], 1)
        gz[0] = jnp.concatenate(
            [jnp.concatenate([wide[:, :256], wide[:, 256:]], 0), jnp.concatenate([rope, jnp.zeros((8, DH), F32)], 0)], 1
        ).astype(BF16)
        pl.semaphore_wait(barrier, len(peers))
        for k in range(7, 0, -1):
            remote(gz.at[0], gz.at[k], gz_send, gz_recv.at[k // 5], at_z(8 - OVER_Z[k])).start()

        def forward(first, count):
            for b in range(1, 8):
                dx, dy = OVER_XY[b]
                blocks = pl.ds(first, count)
                remote(
                    gz.at[blocks, :, pl.ds(0, 256)], gl.at[b, blocks], gl_send, gl_recv.at[b // 4], at_xy(4 - dx, 4 - dy)
                ).start()

        def unpack(first, count):
            block = gl[first : first + count].astype(F32)
            block = jnp.concatenate([block[:, :, :8], block[:, :, 8:]], 3)
            lat[first : first + count, :, :DC] = block.reshape(count, 64, DC).astype(BF16)
            for b in range(first, first + count):
                rope = gr[b].astype(F32)
                rope = jnp.concatenate([rope[:, :DR], rope[:, DR:]], 0)
                lat[b, :, DC:] = jnp.concatenate([rope, jnp.zeros((64, DH - DR), F32)], 1).astype(BF16)

        forward(0, 1)
        loads[2].wait()
        loads[3].wait()
        lat[8:12, :, :DC] = clat[...].reshape(4, 64, DC)
        rope = jnp.concatenate([crope[...].astype(F32).T, jnp.zeros((CLEN, WIDE - DC - DR), F32)], 1)
        lat[8:12, :, DC:] = rope.astype(BF16).reshape(4, 64, WIDE - DC)
        loads[4].wait()
        loads[5].wait()
        project(8, 4)
        place(8, 4)
        arrived(gz.at[pl.ds(1, 4)], gz_recv.at[0])
        forward(1, 4)
        lacc[...] = jnp.zeros_like(lacc)
        racc[...] = jnp.zeros_like(racc)
        arrived(gz.at[pl.ds(5, 3)], gz_recv.at[1])
        forward(5, 3)
        rope = gz[:, :, 256:].astype(F32)[:, :8, :DR].reshape(64, DR)
        gr[0] = jnp.concatenate([rope[:32], rope[32:]], 1).astype(BF16)
        for b in range(1, 8):
            dx, dy = OVER_XY[b]
            remote(gr.at[0], gr.at[b], gr_send, gr_recv.at[b // 4], at_xy(4 - dx, 4 - dy)).start()
        gl[0] = gz[:, :, :256]
        for copy in loads[6:]:
            copy.wait()
        live = lax.broadcasted_iota(jnp.int32, g_ref.shape, 0) < len_ref[...]
        g_ref[...] = jnp.where(live, g_ref[...], jnp.zeros((), BF16))
        arrived(gl.at[pl.ds(1, 3)], gl_recv.at[0])
        arrived(gr.at[pl.ds(1, 3)], gr_recv.at[0])
        unpack(0, 4)
        project(0, 4)
        place(0, 4)
        arrived(gl.at[pl.ds(4, 4)], gl_recv.at[1])
        arrived(gr.at[pl.ds(4, 4)], gr_recv.at[1])
        unpack(4, 4)
        project(4, 4, (0,))
        place(4, 4)
        arrived(gz.at[pl.ds(1, 7)], gz_send)
        arrived(gl.at[pl.ds(1, 7)], gl_send)
        arrived(gr.at[pl.ds(1, 7)], gr_send)

    def weights_of(i, dkv):
        part = jnp.dot(lat_t[...], dkv[...], preferred_element_type=F32).astype(BF16)
        wpart[i] = part.reshape(2, 2, 4, 2, 16, 512)

    def latents_of(i, dkv):
        cols = pl.ds(pl.multiple_of(i * 256, 256), 256)
        both = jnp.concatenate([wk_ref[:, cols], wv_ref[:, cols]], 1)
        lacc[...] += lax.dot_general(dkv[:PLEN], both, NT, preferred_element_type=F32)

    def add_core(i):
        swap_core(i).wait()
        for lo in range(2):
            total = wpart[i, lo, core].astype(F32) + crecv[i, lo].astype(F32)
            csum[i, 0, lo] = total[..., :256].astype(BF16)
            csum[i, 1, lo] = total[..., 256:].astype(BF16)
        for d in (1, 2, 3):
            to = lax.rem(x + d, 4)
            remote(csum.at[i, 0, lax.rem(to, 2), :, lax.div(to, 2)], krecv1.at[i, d - 1], k1_send.at[i], k1_recv.at[i], at_xy(d, 0)).start()
            remote(csum.at[i, 1, :, lax.rem(y + d, 4)], vrecv1.at[i, d - 1], v1_send.at[i], v1_recv.at[i], at_xy(0, d)).start()

    def add_first(i):
        arrived(krecv1.at[i], k1_recv.at[i])
        arrived(vrecv1.at[i], v1_recv.at[i])
        k = csum[i, 0, x_lo, :, x_hi].astype(F32)
        v = csum[i, 1, :, y].astype(F32)
        for d in range(3):
            k = k + krecv1[i, d].astype(F32)
            v = v + vrecv1[i, d].astype(F32)
        ksum[i] = k.astype(BF16)
        vsum[i] = v.astype(BF16)
        for d in (1, 2, 3):
            to = lax.rem(x + d, 4)
            remote(ksum.at[i, lax.rem(y + d, 4)], krecv2.at[i, d - 1], k2_send.at[i], k2_recv.at[i], at_xy(0, d)).start()
            remote(vsum.at[i, lax.rem(to, 2), lax.div(to, 2)], vrecv2.at[i, d - 1], v2_send.at[i], v2_recv.at[i], at_xy(d, 0)).start()

    def add_owned(i):
        arrived(krecv2.at[i], k2_recv.at[i])
        arrived(vrecv2.at[i], v2_recv.at[i])
        k = ksum[i, y].astype(F32)
        v = vsum[i, x_lo, x_hi].astype(F32)
        for d in range(3):
            k = k + krecv2[i, d].astype(F32)
            v = v + vrecv2[i, d].astype(F32)
        cols = pl.ds(pl.multiple_of(i * 256, 256), 256)
        gw_ref[0, :, cols] = k
        gw_ref[1, :, cols] = v
        arrived(krecv1.at[i], k1_send.at[i])
        arrived(vrecv1.at[i], v1_send.at[i])
        arrived(krecv2.at[i], k2_send.at[i])
        arrived(vrecv2.at[i], v2_send.at[i])

    see = lax.broadcasted_iota(jnp.int32, (CLEN, CLEN), 0) <= lax.broadcasted_iota(jnp.int32, (CLEN, CLEN), 1)

    last = PAIRS - 1

    def scores(i, h):
        mine = pl.ds(pl.multiple_of(i * 256 + h * DH, DH), DH)
        cols = slice(h * DH, (h + 1) * DH)
        kx = jnp.concatenate([kv[i, 0, :, cols], rsel[h]], 1)
        qx = jnp.concatenate([q_ref[:, mine], qr_ref[:, pl.ds(pl.multiple_of(i * DH, DH), DH)]], 1)
        g = g_ref[:, mine]
        s = lax.dot_general(kx, qx, NT, preferred_element_type=F32)
        dprob = lax.dot_general(kv[i, 1, :, cols], g, NT, preferred_element_type=F32)
        return qx, g, s, dprob

    def gradients(h, new, qx, g, s, dprob):
        s = jnp.concatenate([s[:PLEN], jnp.where(see, s[PLEN:], -1e30)], 0)
        m = jnp.max(s, axis=0, keepdims=True)
        p = jnp.exp2((s - m) * (SCALE * math.log2(math.e)))
        p = p * (1.0 / jnp.sum(p, axis=0, keepdims=True))
        pb = p.astype(BF16)
        new[:, 256 + h * DH : 256 + (h + 1) * DH] = jnp.dot(pb, g, preferred_element_type=F32).astype(BF16)
        delta = jnp.sum(pb.astype(F32) * dprob, axis=0, keepdims=True)
        ds = (p * (dprob - delta)).astype(BF16)
        dk = jnp.dot(ds, qx, preferred_element_type=F32)
        new[:, h * DH : (h + 1) * DH] = (dk[:, :DH] * SCALE).astype(BF16)
        racc[h] += dk[:PLEN, DH:]

    def attend(i, new, before, old):
        one = scores(i, 0)
        weights_of(before, old)
        two = scores(i, 1)
        latents_of(before, old)
        gradients(0, new, *one)
        gradients(1, new, *two)

    def grads_of_head(h):
        return jnp.concatenate([dkv_b[:, h * DH : (h + 1) * DH], dkv_b[:, 256 + h * DH : 256 + (h + 1) * DH]], 1)

    def weights_of_head(h):
        part = jnp.dot(lat_t[...], grads_of_head(h), preferred_element_type=F32).astype(BF16)
        for n in range(2):
            cols = slice(n * 256 + h * DH, n * 256 + (h + 1) * DH)
            wpart[last, :, :, :, :, :, cols] = part[:, n * DH : (n + 1) * DH].reshape(2, 2, 4, 2, 16, DH)

    def latents_of_head(h):
        mine = slice(last * 256 + h * DH, last * 256 + (h + 1) * DH)
        both = jnp.concatenate([wk_ref[:, mine], wv_ref[:, mine]], 1)
        lacc[...] += lax.dot_general(grads_of_head(h)[:PLEN], both, NT, preferred_element_type=F32)

    first, second = 2 * step, 2 * step + 1

    @pl.when(step == 0)
    def _():
        one = scores(0, 0)
        two = scores(0, 1)
        project(4, 4, range(1, PAIRS))
        gradients(0, dkv_a, *one)
        gradients(1, dkv_a, *two)

    @pl.when(step >= 1)
    def _():
        attend(first, dkv_a, first - 1, dkv_b)
        swap_core(first - 1).start()
        add_core(first - 2)

    @pl.when(step >= 2)
    def _():
        add_first(first - 4)

    @pl.when(step >= 3)
    def _():
        add_owned(first - 6)

    @pl.when(step < STEPS - 1)
    def _():
        attend(second, dkv_b, first, dkv_a)
        swap_core(first).start()

    @pl.when((step >= 1) & (step < STEPS - 1))
    def _():
        add_core(first - 1)

    @pl.when((step >= 2) & (step < STEPS - 1))
    def _():
        add_first(first - 3)

    @pl.when(step == STEPS - 1)
    def _():
        head = scores(last, 0)
        weights_of(last - 1, dkv_a)
        latents_of(last - 1, dkv_a)
        gradients(0, dkv_b, *head)
        swap_core(last - 1).start()
        add_core(last - 2)
        add_first(last - 4)

    @pl.when(step == STEPS - 1)
    def _():
        head = scores(last, 1)
        weights_of_head(0)
        latents_of_head(0)
        gradients(1, dkv_b, *head)

    @pl.when(step == STEPS - 1)
    def _():
        latents_of_head(1)
        apart[...] = lacc[:, :ACOLS].astype(BF16).reshape(8, 64, ACOLS)
        for b in range(1, 8):
            remote(apart.at[b], a1recv.at[b - 1], a1_send, a1_recv, at_xy(*OVER_XY[b])).start()
        weights_of_head(1)
        swap_core(last).start()
        add_core(last - 1)
        rope = (racc[0, :, :DR] + racc[1, :, DR:]) * SCALE
        rest = lacc[:, ACOLS:]
        for k in range(8):
            mine = [slice(b * 64 + k * 8, b * 64 + k * 8 + 8) for b in range(8)]
            left = jnp.concatenate([rope[rows] for rows in mine[:4]], 0)
            right = jnp.concatenate([rope[rows] for rows in mine[4:]], 0)
            both = jnp.concatenate([left, right], 1)
            bpart[k] = jnp.concatenate([rest[rows] for rows in mine] + [both], 0).astype(BF16)
        for k in range(7, 0, -1):
            remote(bpart.at[k], b1recv.at[k - 1], b1_send, b1_recv, at_z(OVER_Z[k])).start()
        add_core(last)
        add_first(last - 3)
        add_owned(last - 6)
        add_owned(last - 5)
        add_first(last - 2)
        arrived(a1recv, a1_recv)
        total = apart[0].astype(F32)
        for b in range(7):
            total = total + a1recv[b].astype(F32)
        total = total.reshape(8, 8, ACOLS)
        a2own[...] = total[0]
        right = jnp.concatenate([total[:, :, 256:], jnp.zeros((8, 8, 512 - ACOLS), F32)], 2)
        a2src[...] = jnp.concatenate([total[:, :, :256], right], 1).astype(BF16)
        for k in range(7, 0, -1):
            remote(a2src.at[k], a2recv.at[k - 1], a2_send, a2_recv, at_z(OVER_Z[k])).start()
        add_first(last - 1)
        add_first(last)
        arrived(b1recv, b1_recv)
        total = bpart[0].astype(F32)
        for k in range(7):
            total = total + b1recv[k].astype(F32)
        rope = jnp.concatenate([total[64:, :DR], total[64:, DR:]], 0)
        rope = jnp.concatenate([rope, jnp.zeros((64, DH - DR), F32)], 1)
        b2src[...] = jnp.concatenate([total[:64], rope], 1).reshape(8, 8, BCOLS)
        for b in range(1, 8):
            remote(b2src.at[b], b2recv.at[b - 1], b2_send, b2_recv, at_xy(*OVER_XY[b])).start()
        lax.fori_loop(last - 4, last + 1, lambda i, c: (add_owned(i), c)[1], 0)
        arrived(a2recv, a2_recv)
        total = a2recv[0].astype(F32)
        for k in range(1, 7):
            total = total + a2recv[k].astype(F32)
        glat_ref[:, :256] = a2own[:, :256] + total[:8]
        glat_ref[:, 256:ACOLS] = a2own[:, 256:] + total[8:, : ACOLS - 256]
        arrived(b2recv, b2_recv)
        total = b2src[0]
        for b in range(7):
            total = total + b2recv[b]
        glat_ref[:, ACOLS:] = total
        arrived(a1recv, a1_send)
        arrived(b1recv, b1_send)
        arrived(a2recv, a2_send)
        arrived(b2recv, b2_send)


def finish(lat_ref, w_ref, glat_ref, grope_ref, gwk_ref, gwv_ref):
    glat_ref[...] = lat_ref[:, :DC]
    grope_ref[...] = lat_ref[:, DC : DC + DR]
    gwk_ref[...] = w_ref[0]
    gwv_ref[...] = w_ref[1]


def local(prompt_latent, prompt_rope, comp_latent, comp_rope, query_nope, query_rope, grad_out, lengths, w_uk, w_uv):
    def whole(*shape):
        return pl.BlockSpec(shape, lambda i: (0,) * len(shape))

    vmem, dma = pltpu.VMEM, pltpu.SemaphoreType.DMA
    lat, weights = pl.pallas_call(
        kernel,
        grid=(STEPS,),
        in_specs=[pl.BlockSpec(memory_space=pl.ANY)] * 10,
        out_specs=[whole(8, WIDE), whole(2, 16, 2048)],
        out_shape=[jax.ShapeDtypeStruct((8, WIDE), F32), jax.ShapeDtypeStruct((2, 16, 2048), F32)],
        scratch_shapes=[
            vmem((8, DC), BF16), vmem((8, DR), BF16), vmem((CLEN, DC), BF16), vmem((DR, CLEN), BF16),
            vmem((CLEN, 2048), BF16), vmem((CLEN, 1024), BF16), vmem((CLEN, 2048), BF16),
            vmem((DC, 2048), BF16), vmem((DC, 2048), BF16), vmem((1, 1), jnp.int32),
            vmem((8, 16, PACK), BF16), vmem((8, 8, 16, 256), BF16), vmem((8, 32, DH), BF16),
            vmem((12, 64, WIDE), BF16), vmem((DC, KEYS), BF16), vmem((2, KEYS, DH), BF16),
            vmem((PAIRS, 2, KEYS, 256), BF16), vmem((KEYS, 512), BF16), vmem((KEYS, 512), BF16),
            vmem((PLEN, DC), F32), vmem((2, PLEN, DH), F32),
            vmem((PAIRS, 2, 2, 4, 2, 16, 512), BF16),
            vmem((PAIRS, 2, 4, 2, 16, 512), BF16),
            vmem((PAIRS, 2, 2, 4, 2, 16, 256), BF16),
            vmem((PAIRS, 3, 4, 16, 256), BF16), vmem((PAIRS, 4, 16, 256), BF16), vmem((PAIRS, 3, 16, 256), BF16),
            vmem((PAIRS, 3, 2, 2, 16, 256), BF16), vmem((PAIRS, 2, 2, 16, 256), BF16), vmem((PAIRS, 3, 16, 256), BF16),
            vmem((8, 64, ACOLS), BF16), vmem((7, 64, ACOLS), BF16), vmem((8, 16, 256), BF16), vmem((8, ACOLS), F32), vmem((7, 16, 256), BF16),
            vmem((8, 96, DH), BF16), vmem((7, 96, DH), BF16), vmem((8, 8, BCOLS), F32), vmem((7, 8, BCOLS), F32),
            dma((10,)), dma, dma((2,)), dma, dma((2,)), dma, dma((2,)),
            *[dma((PAIRS,))] * 10, *[dma] * 8,
        ],
        compiler_params=pltpu.CompilerParams(
            vmem_limit_bytes=56 * 1024 * 1024, collective_id=0, has_side_effects=True
        ),
        cost_estimate=pl.CostEstimate(flops=13_000_000_000, bytes_accessed=8_000_000, transcendentals=3_200_000),
        name="mla_backward",
    )(
        lengths, prompt_latent[0], prompt_rope[0], comp_latent[0, 0], comp_rope[0, 0].T,
        query_nope[0, 0], query_rope[0, 0], grad_out[0, 0], w_uk, w_uv,
    )
    outs = pl.pallas_call(
        finish,
        out_shape=[
            jax.ShapeDtypeStruct((8, DC), F32), jax.ShapeDtypeStruct((8, DR), F32),
            jax.ShapeDtypeStruct((16, 2048), F32), jax.ShapeDtypeStruct((16, 2048), F32),
        ],
        name="outputs",
    )(lat, weights)
    return (outs[0][None], outs[1][None], outs[2], outs[3])


def solution(mesh):
    in_specs = (
        P("dp", ("sample", "head"), None),
        P("dp", ("sample", "head"), None),
        P("dp", "sample", None, None),
        P("dp", "sample", None, None),
        P("dp", "sample", None, "head"),
        P("dp", "sample", None, "head"),
        P("dp", "sample", None, "head"),
        P("dp", "sample"),
        P(None, "head"),
        P(None, "head"),
    )
    out_specs = (
        P("dp", ("sample", "head"), None),
        P("dp", ("sample", "head"), None),
        P(("dp", "sample"), "head"),
        P(("dp", "sample"), "head"),
    )
    return jax.shard_map(local, mesh=mesh, in_specs=in_specs, out_specs=out_specs, check_vma=False)
```
